32 devices in a mesh: groups: 2 (over y), node: 4 (over z), local: 4 (over x, core).
Axes of the slice: x: 2, y: 2, z: 4, core: 2. Of those that a mesh axis runs over, the one named last changes fastest.
Arguments:
- hidden_states: bfloat16 [128, 3584], P(('groups', 'node', 'local')), parts along dimension 0, may hold values from -6 to 6
- norm_gain: float32 [3584], replicated, may hold values from 0.5 to 1.5
- route_groups: int32 [128, 4], P(('groups', 'node', 'local')), parts along dimension 0, may hold values from 0 to 7, as said below
- route_picks: int32 [128, 8], P(('groups', 'node', 'local')), parts along dimension 0, may hold values from 0 to 15, as said below
- gate_weights: bfloat16 [128, 8], P(('groups', 'node', 'local')), parts along dimension 0, may hold values from 0.049804688 to 0.5
- expert_gate: bfloat16 [32, 3584, 1024], P('node', None, 'local'), may hold values from -0.09375 to 0.09375
- expert_up: bfloat16 [32, 3584, 1024], P('node', None, 'local'), may hold values from -0.09375 to 0.09375
- expert_down: bfloat16 [32, 1024, 3584], P('node', 'local'), may hold values from -0.1875 to 0.1875
- shared_gate: bfloat16 [1024, 3584], P('local', 'node'), may hold values from -0.09375 to 0.09375
- shared_up: bfloat16 [1024, 3584], P('local', 'node'), may hold values from -0.09375 to 0.09375
- shared_down: bfloat16 [1024, 3584], P('local', 'node'), may hold values from -0.1875 to 0.1875
Outputs:
- moe_out: bfloat16 [128, 3584], P(('groups', 'node', 'local')), parts along dimension 0
The draws below stay inside these ranges and needn't reach their ends.
There are 2 independent parts, one for each index of `groups`. The reference program is written for one: setup_inputs(seed, part) draws one part's arguments, and reference() takes and returns one part's arrays. A program takes and returns all parts, laid end to end along the dimension named above; an argument that names none is the same for every part. Nothing has to cross between parts.
Inputs may be any that keep to these rules, and one draw needn't show every extreme that they name: `route_groups`: each row names 4 different node groups; the 4 tokens of every device name each node group exactly 2 times. `route_picks`: each row holds 8 different values; the value a * 4 + j picks expert route_groups[t, a] * 4 + j, and every a from 0 to 3 appears in 2 values of every row; of one device's tokens at most 2 pick any one expert, and in every draw some expert is picked by exactly 2 tokens of every device.
All inputs are finite; a program needn't handle non-finite values.
Results may differ from the reference program's by a relative error of at most 0.012.
Values may be sent and summed in bfloat16 or wider, within the bound.
No kernel may reach another device: no remote copies, remote signals or barrier semaphores. Data moves between devices by JAX's collectives and lax.ppermute only.
A program may use at most 128 MiB of HBM per device.

```python
import math
import jax
import jax.numpy as jnp
from jax import lax

D = 3584
FH = 1024
SH = 1024
TOP_K = 8
NODE_GROUPS = 8
TOP_GROUPS = 4
EXPERTS = 32
PER_GROUP = 4
TOK_DEV = 4
CAP = 2
TOKENS = 64
N_LOCAL = 4


def route_plan(key):
    device_count = TOKENS // TOK_DEV
    order_key = jax.random.fold_in(key, 101)
    scores = jax.random.randint(order_key, (device_count, CAP, NODE_GROUPS), 0, 2 ** 20) * NODE_GROUPS + jnp.arange(NODE_GROUPS, dtype=jnp.int32)
    ordering = jnp.argsort(scores, axis=-1).astype(jnp.int32)
    groups_drawn = ordering.reshape(TOKENS, TOP_GROUPS)
    favored = jax.random.randint(jax.random.fold_in(key, 102), (NODE_GROUPS,), 0, PER_GROUP).astype(jnp.int32)
    favored_slot = favored[groups_drawn]
    pick_scores = jax.random.randint(jax.random.fold_in(key, 103), (TOKENS, TOP_GROUPS, PER_GROUP), 0, 2 ** 20) * PER_GROUP + jnp.arange(PER_GROUP, dtype=jnp.int32)
    boosted = jnp.where(jnp.arange(PER_GROUP, dtype=jnp.int32)[None, None, :] == favored_slot[:, :, None], pick_scores + 2 ** 26, pick_scores)
    inner = lax.top_k(boosted, TOP_K // TOP_GROUPS)[1].astype(jnp.int32)
    picks = jnp.arange(TOP_GROUPS, dtype=jnp.int32)[None, :, None] * PER_GROUP + inner
    return (groups_drawn.astype(jnp.int32), picks.reshape(TOKENS, TOP_K).astype(jnp.int32))


def draw_route_groups(key, part):
    planned = route_plan(key)
    return planned[0]


def draw_route_picks(key, part):
    planned = route_plan(key)
    return planned[1]


def block_levels(rng, shape, split, low, high):
    def one(position, shards_of):
        heights = jax.random.uniform(jax.random.fold_in(jax.random.fold_in(rng, 6), position), (shards_of,), jnp.float32, low / len(split), high / len(split))
        return jnp.repeat(jnp.exp(heights), shape[position] // shards_of).reshape((-1,) + (1,) * (len(shape) - position - 1))

    level = one(*split[0])
    for cut in split[1:]:
        level = level * one(*cut)
    return level


def centred(key, extent, width, most, pieces=(), kind=jnp.bfloat16):
    values = jax.random.normal(key, extent, jnp.float32) * width
    if len(pieces) > 0:
        values = block_levels(key, extent, pieces, -0.22, 0.18) * values
    return jnp.clip(values, min=-most, max=most).astype(kind)


def setup_inputs(seed: int = 0, part: int = 0) -> dict:
    seeds = jax.random.split(jax.random.key(seed), 12)
    part_keys = jax.random.split(jax.random.fold_in(seeds[11], part), 12)
    return {
        "hidden_states": centred(part_keys[0], (TOKENS, D), 1.0, 6.0, ((0, 16),)),
        "norm_gain": jnp.clip(1.0 + 0.1 * jax.random.normal(seeds[1], (D,), jnp.float32), 0.5, 1.5),
        "route_groups": draw_route_groups(jax.random.fold_in(jax.random.fold_in(seeds[11], part), 71), part),
        "route_picks": draw_route_picks(jax.random.fold_in(jax.random.fold_in(seeds[11], part), 71), part),
        "gate_weights": jnp.clip(jnp.exp(math.log(0.5) - 2.306499 * jax.random.uniform(part_keys[4], (TOKENS, TOP_K), jnp.float32) ** block_levels(part_keys[4], (TOKENS, TOP_K), ((0, 16),), -0.2, 0.2)), 0.049804688, 0.5).astype(jnp.bfloat16),
        "expert_gate": centred(seeds[5], (EXPERTS, D, FH), D ** -0.5, 0.09375, ((0, 4), (2, 4))),
        "expert_up": centred(seeds[6], (EXPERTS, D, FH), D ** -0.5, 0.09375, ((0, 4), (2, 4))),
        "expert_down": centred(seeds[7], (EXPERTS, FH, D), FH ** -0.5, 0.1875, ((0, 4), (1, 4))),
        "shared_gate": centred(seeds[8], (SH, D), D ** -0.5, 0.09375, ((0, 4), (1, 4))),
        "shared_up": centred(seeds[9], (SH, D), D ** -0.5, 0.09375, ((0, 4), (1, 4))),
        "shared_down": centred(seeds[10], (SH, D), SH ** -0.5, 0.1875, ((0, 4), (1, 4))),
    }


def reference(hidden_states, norm_gain, route_groups, route_picks, gate_weights, expert_gate, expert_up, expert_down, shared_gate, shared_up, shared_down):
    features = hidden_states.astype(jnp.float32)
    mean_square = lax.optimization_barrier(jnp.mean(features * features, axis=1, keepdims=True))
    normed = (features * lax.rsqrt(mean_square + 1e-06) * norm_gain[None, :]).astype(jnp.bfloat16)
    group_slot = (route_picks // PER_GROUP).astype(jnp.int32)
    inner_pick = (route_picks % PER_GROUP).astype(jnp.int32)
    group_pick = jnp.take_along_axis(route_groups, group_slot, axis=1)
    expert_ids = (group_pick * PER_GROUP + inner_pick).astype(jnp.int32)
    weights_float = gate_weights.astype(jnp.float32)
    block = FH // N_LOCAL

    def per_expert(totals, expert_number):
        row_weight = lax.optimization_barrier(jnp.sum(jnp.where(expert_ids == expert_number, weights_float, 0.0), axis=1))
        gate_matrix = lax.dynamic_index_in_dim(expert_gate, expert_number, 0, keepdims=False)
        up_matrix = lax.dynamic_index_in_dim(expert_up, expert_number, 0, keepdims=False)
        down_matrix = lax.dynamic_index_in_dim(expert_down, expert_number, 0, keepdims=False)
        term = jnp.zeros((TOKENS, D), jnp.float32)
        for index in range(N_LOCAL):
            gate_part = jnp.dot(normed, gate_matrix[:, index * block:(index + 1) * block], preferred_element_type=jnp.float32)
            up_part = jnp.dot(normed, up_matrix[:, index * block:(index + 1) * block], preferred_element_type=jnp.float32)
            block_hidden = (jax.nn.silu(gate_part) * up_part).astype(jnp.bfloat16)
            output = jnp.dot(block_hidden, down_matrix[index * block:(index + 1) * block, :], preferred_element_type=jnp.float32)
            block_term = lax.optimization_barrier((row_weight[:, None] * output).astype(jnp.bfloat16))
            term = term + block_term.astype(jnp.float32)
        routed_term = lax.optimization_barrier(term.astype(jnp.bfloat16))
        return (totals + routed_term.astype(jnp.float32), None)
    routed, unused = lax.scan(per_expert, jnp.zeros((TOKENS, D), jnp.float32), jnp.arange(EXPERTS, dtype=jnp.int32))
    contract = (((1,), (1,)), ((), ()))
    shared_block = SH // N_LOCAL
    shared_out = jnp.zeros((TOKENS, D), jnp.float32)
    for index in range(N_LOCAL):
        rows = slice(index * shared_block, (index + 1) * shared_block)
        gate_part = lax.dot_general(normed, shared_gate[rows], contract, preferred_element_type=jnp.float32)
        up_part = lax.dot_general(normed, shared_up[rows], contract, preferred_element_type=jnp.float32)
        shared_hidden = (jax.nn.silu(gate_part) * up_part).astype(jnp.bfloat16)
        shared_term = lax.optimization_barrier(jnp.dot(shared_hidden, shared_down[rows], preferred_element_type=jnp.float32).astype(jnp.bfloat16))
        shared_out = shared_out + shared_term.astype(jnp.float32)
    return (shared_out + routed).astype(jnp.bfloat16)
```

```python
import jax
import jax.numpy as jnp
from jax import lax
from jax.sharding import PartitionSpec as P

NODE_GROUPS = 8


def local(
    hidden_states,
    norm_gain,
    route_groups,
    route_picks,
    gate_weights,
    expert_gate,
    expert_up,
    expert_down,
    shared_gate,
    shared_up,
    shared_down,
):
    node_count = lax.axis_size("node")
    local_count = lax.axis_size("local")
    node = lax.axis_index("node")
    token_count, feature_count = hidden_states.shape
    held, _, block = expert_gate.shape
    expert_total = held * node_count
    per_group = expert_total // NODE_GROUPS
    features = hidden_states.astype(jnp.float32)
    mean_square = jnp.mean(features * features, axis=1, keepdims=True)
    normed = (features * lax.rsqrt(mean_square + 1e-06) * norm_gain[None, :]).astype(jnp.bfloat16)
    group_pick = jnp.take_along_axis(route_groups, route_picks // per_group, axis=1)
    expert_ids = group_pick * per_group + route_picks % per_group
    hits = expert_ids[:, :, None] == jnp.arange(expert_total, dtype=jnp.int32)[None, None, :]
    token_weight = jnp.sum(
        jnp.where(hits, gate_weights.astype(jnp.float32)[:, :, None], 0.0), axis=1
    ).astype(jnp.bfloat16)
    packed = jnp.concatenate([normed, token_weight], axis=1)
    gathered = lax.all_gather(packed, ("node", "local"), axis=0, tiled=True)
    rows = gathered[:, :feature_count]
    weights = lax.dynamic_slice_in_dim(gathered, feature_count + node * held, held, axis=1)
    weights = weights.astype(jnp.float32)
    slab = shared_gate.shape[1]
    mine = lax.dynamic_slice_in_dim(rows, node * slab, slab, axis=1)
    contract = (((1,), (1,)), ((), ()))
    shared_parts = jnp.concatenate(
        [
            lax.dot_general(mine, shared_gate, contract, preferred_element_type=jnp.float32),
            lax.dot_general(mine, shared_up, contract, preferred_element_type=jnp.float32),
        ],
        axis=1,
    )
    shared_parts = lax.all_gather(shared_parts.astype(jnp.bfloat16), "node", axis=0, tiled=False)
    shared_in = jnp.sum(shared_parts.astype(jnp.float32), axis=0)
    shared_block = shared_gate.shape[0]
    shared_hidden = (
        jax.nn.silu(shared_in[:, :shared_block]) * shared_in[:, shared_block:]
    ).astype(jnp.bfloat16)
    hidden = []
    for e in range(held):
        gate_part = jnp.dot(rows, expert_gate[e], preferred_element_type=jnp.float32)
        up_part = jnp.dot(rows, expert_up[e], preferred_element_type=jnp.float32)
        hidden.append(
            (jax.nn.silu(gate_part) * up_part * weights[:, e : e + 1]).astype(jnp.bfloat16)
        )
    hidden = jnp.concatenate(hidden, axis=1)
    partial = jnp.dot(
        hidden,
        expert_down.reshape(held * block, feature_count),
        preferred_element_type=jnp.float32,
    )
    shared_partial = jnp.dot(shared_hidden, shared_down, preferred_element_type=jnp.float32)
    current = lax.dynamic_slice_in_dim(partial, node * slab, slab, axis=1)
    partial = lax.dynamic_update_slice_in_dim(
        partial, current + shared_partial, node * slab, axis=1
    ).astype(jnp.bfloat16)
    stack = partial.reshape(node_count * local_count, token_count, feature_count)
    returned = lax.all_to_all(stack, ("node", "local"), split_axis=0, concat_axis=0, tiled=True)
    return jnp.sum(returned.astype(jnp.float32), axis=0).astype(jnp.bfloat16)


def solution(mesh):
    placed = (
        P(("groups", "node", "local"), None),
        P(),
        P(("groups", "node", "local"), None),
        P(("groups", "node", "local"), None),
        P(("groups", "node", "local"), None),
        P("node", None, "local"),
        P("node", None, "local"),
        P("node", "local", None),
        P("local", "node"),
        P("local", "node"),
        P("local", "node"),
    )
    return jax.shard_map(
        local,
        mesh=mesh,
        in_specs=placed,
        out_specs=P(("groups", "node", "local"), None),
        check_vma=False,
    )
```

```python
import functools

import jax
import jax.numpy as jnp
from jax import lax
from jax.experimental import pallas as pl
from jax.experimental.pallas import tpu as pltpu
from jax.sharding import PartitionSpec as P

NODE_GROUPS = 8
LANES = 128
VMEM_BYTES = 56 * 2**20


def pack_kernel(per_group, x_ref, gain_ref, groups_ref, picks_ref, weight_ref, out_ref):
    features = x_ref[...].astype(jnp.float32)
    count = features.shape[1]
    mean_square = jnp.mean(features * features, axis=1, keepdims=True)
    normed = features * lax.rsqrt(mean_square + 1e-06) * gain_ref[...]
    out_ref[:, :count] = normed.astype(jnp.bfloat16)
    picks = picks_ref[...]
    groups = groups_ref[...]
    weight = weight_ref[...].astype(jnp.float32)
    slot = lax.div(picks, jnp.full_like(picks, per_group))
    inner = picks - slot * per_group
    group = jnp.zeros_like(picks)
    for a in range(groups.shape[1]):
        group = jnp.where(slot == a, groups[:, a : a + 1], group)
    ids = group * per_group + inner
    width = out_ref.shape[1] - count
    lane = lax.broadcasted_iota(jnp.int32, (picks.shape[0], width), 1)
    total = jnp.zeros((picks.shape[0], width), jnp.float32)
    for k in range(picks.shape[1]):
        total = total + jnp.where(ids[:, k : k + 1] == lane, weight[:, k : k + 1], 0.0)
    out_ref[:, count:] = total.astype(jnp.bfloat16)


def shared_in_kernel(start_ref, x_ref, gate_ref, up_ref, out_ref):
    contract = (((1,), (1,)), ((), ()))
    block, slab = gate_ref.shape
    x = x_ref[...]
    if x.shape[1] != slab:
        x = x_ref[:, pl.ds(pl.multiple_of(start_ref[0], LANES), slab)]
    for i, ref in enumerate((gate_ref, up_ref)):
        part = lax.dot_general(x, ref[...], contract, preferred_element_type=jnp.float32)
        out_ref[:, i * block : (i + 1) * block] = part.astype(jnp.bfloat16)


def hidden_kernel(first_ref, x_ref, gate_ref, up_ref, out_ref):
    count = gate_ref.shape[1]
    x = x_ref[:, :count]
    gate = jnp.dot(x, gate_ref[0], preferred_element_type=jnp.float32)
    up = jnp.dot(x, up_ref[0], preferred_element_type=jnp.float32)
    weight = x_ref[:, count:].astype(jnp.float32)
    lane = lax.broadcasted_iota(jnp.int32, weight.shape, 1)
    chosen = first_ref[0] + pl.program_id(0)
    weight = jnp.sum(jnp.where(lane == chosen, weight, 0.0), axis=1, keepdims=True)
    out_ref[...] = (jax.nn.silu(gate) * up * weight).astype(jnp.bfloat16)


def down_kernel(tokens, start_ref, hidden_ref, down_ref, shared_down_ref, *refs):
    parts, out_ref, acc = refs[:-2], refs[-2], refs[-1]
    step = pl.program_id(0)
    term = jnp.dot(hidden_ref[...], down_ref[0], preferred_element_type=jnp.float32)

    @pl.when(step == 0)
    def _():
        acc[...] = term

    @pl.when(step > 0)
    def _():
        acc[...] += term

    @pl.when(step == pl.num_programs(0) - 1)
    def _():
        block, slab = shared_down_ref.shape
        count = out_ref.shape[0]
        total = parts[0][...].astype(jnp.float32)
        to = lax.broadcasted_iota(jnp.int32, (count, count), 0)
        come = lax.broadcasted_iota(jnp.int32, (count, count), 1)
        for k in range(1, len(parts)):
            place = (come == (to ^ (k * tokens))).astype(jnp.bfloat16)
            total += jnp.dot(place, parts[k][...], preferred_element_type=jnp.float32)
        hidden = (jax.nn.silu(total[:, :block]) * total[:, block:]).astype(jnp.bfloat16)
        shared = jnp.dot(hidden, shared_down_ref[...], preferred_element_type=jnp.float32)
        if slab == out_ref.shape[1]:
            acc[...] += shared
        else:
            acc[:, pl.ds(pl.multiple_of(start_ref[0], LANES), slab)] += shared
        out_ref[...] = acc[...].astype(jnp.bfloat16)


def exchange(value, axis, bit):
    size = lax.axis_size(axis)
    return lax.ppermute(value, axis, [(i, i ^ bit) for i in range(size)])


def add_rows(one, other):
    return (one.astype(jnp.float32) + other.astype(jnp.float32)).astype(jnp.bfloat16)


def local(
    hidden_states,
    norm_gain,
    route_groups,
    route_picks,
    gate_weights,
    expert_gate,
    expert_up,
    expert_down,
    shared_gate,
    shared_up,
    shared_down,
):
    node_count = lax.axis_size("node")
    local_count = lax.axis_size("local")
    node = lax.axis_index("node")
    token_count, feature_count = hidden_states.shape
    held, _, block = expert_gate.shape
    expert_total = held * node_count
    per_group = expert_total // NODE_GROUPS
    width = feature_count + -(-expert_total // LANES) * LANES
    slab = shared_gate.shape[1]
    shared_block = shared_gate.shape[0]
    params = pltpu.CompilerParams(vmem_limit_bytes=VMEM_BYTES)

    rows = pl.pallas_call(
        functools.partial(pack_kernel, per_group),
        out_shape=jax.ShapeDtypeStruct((token_count, width), jnp.bfloat16),
    )(hidden_states, norm_gain.reshape(1, -1), route_groups, route_picks, gate_weights)

    bit = 1
    while bit < node_count:
        rows = jnp.concatenate([rows, exchange(rows, "node", bit)], axis=0)
        bit *= 2
    bit = local_count // 2
    while bit:
        rows = jnp.concatenate([rows, exchange(rows, "local", bit)], axis=0)
        bit //= 2
    row_count = rows.shape[0]

    start = (node * slab).astype(jnp.int32)
    aligned = slab % LANES == 0
    smem = pl.BlockSpec(memory_space=pltpu.SMEM)
    vmem = pl.BlockSpec(memory_space=pltpu.VMEM)
    mine = rows if aligned else lax.dynamic_slice_in_dim(rows, start, slab, axis=1)
    shared_part = pl.pallas_call(
        shared_in_kernel,
        out_shape=jax.ShapeDtypeStruct((row_count, 2 * shared_block), jnp.bfloat16),
        in_specs=[smem, vmem, vmem, vmem],
        compiler_params=params,
    )(start.reshape(1), mine, shared_gate, shared_up)
    parts = [shared_part] + [exchange(shared_part, "node", k) for k in range(1, node_count)]

    hidden = pl.pallas_call(
        hidden_kernel,
        grid=(held,),
        out_shape=jax.ShapeDtypeStruct((row_count, held * block), jnp.bfloat16),
        in_specs=[
            smem,
            vmem,
            pl.BlockSpec((1, feature_count, block), lambda e: (e, 0, 0)),
            pl.BlockSpec((1, feature_count, block), lambda e: (e, 0, 0)),
        ],
        out_specs=pl.BlockSpec((row_count, block), lambda e: (0, e)),
        compiler_params=params,
    )((node * held).astype(jnp.int32).reshape(1), rows, expert_gate, expert_up)

    if not aligned:
        shared_down = lax.dynamic_update_slice_in_dim(
            jnp.zeros((shared_block, feature_count), shared_down.dtype), shared_down, start, axis=1
        )
    out = pl.pallas_call(
        functools.partial(down_kernel, token_count),
        grid=(held,),
        out_shape=jax.ShapeDtypeStruct((row_count, feature_count), jnp.bfloat16),
        in_specs=[
            smem,
            pl.BlockSpec((row_count, block), lambda e: (0, e)),
            pl.BlockSpec((1, block, feature_count), lambda e: (e, 0, 0)),
            vmem,
        ]
        + [vmem] * node_count,
        out_specs=vmem,
        scratch_shapes=[pltpu.VMEM((row_count, feature_count), jnp.float32)],
        compiler_params=params,
    )(start.reshape(1), hidden, expert_down, shared_down, *parts)

    bit = 1
    while bit < local_count:
        half = out.shape[0] // 2
        out = add_rows(out[:half], exchange(out[half:], "local", bit))
        bit *= 2
    bit = node_count // 2
    while bit:
        half = out.shape[0] // 2
        out = add_rows(out[:half], exchange(out[half:], "node", bit))
        bit //= 2
    return out


def solution(mesh):
    placed = (
        P(("groups", "node", "local"), None),
        P(),
        P(("groups", "node", "local"), None),
        P(("groups", "node", "local"), None),
        P(("groups", "node", "local"), None),
        P("node", None, "local"),
        P("node", None, "local"),
        P("node", "local", None),
        P("local", "node"),
        P("local", "node"),
        P("local", "node"),
    )
    return jax.shard_map(
        local,
        mesh=mesh,
        in_specs=placed,
        out_specs=P(("groups", "node", "local"), None),
        check_vma=False,
    )
```

```python
import functools
import math

import jax
import jax.numpy as jnp
from jax import lax
from jax.experimental import pallas as pl
from jax.experimental.pallas import tpu as pltpu
from jax.sharding import PartitionSpec as P

NODE_GROUPS = 8
LANES = 128
MIB = 2**20
NEAR_PLAN = (0, 0, 0, 1)


def pack_kernel(per_group, *refs):
    count = len(refs) // 2 - 1
    sources, out_ref, staged, sems = refs[:count], refs[count], refs[count + 1 : -1], refs[-1]
    copies = [
        pltpu.make_async_copy(here, there, sems.at[i])
        for i, (here, there) in enumerate(zip(sources, staged))
    ]
    for copy in copies:
        copy.start()
    for copy in copies:
        copy.wait()
    x_ref, gain_ref, groups_ref, picks_ref, weight_ref = staged
    features = x_ref[...].astype(jnp.float32)
    count = features.shape[1]
    mean_square = jnp.mean(features * features, axis=1, keepdims=True)
    normed = features * lax.rsqrt(mean_square + 1e-06) * gain_ref[...].reshape(1, -1)
    out_ref[:, :count] = normed.astype(jnp.bfloat16)
    picks = picks_ref[...]
    groups = groups_ref[...]
    weight = weight_ref[...].astype(jnp.float32)
    slot = lax.div(picks, jnp.full_like(picks, per_group))
    inner = picks - slot * per_group
    group = jnp.zeros_like(picks)
    for a in range(groups.shape[1]):
        group = jnp.where(slot == a, groups[:, a : a + 1], group)
    ids = group * per_group + inner
    width = out_ref.shape[1] - count
    lane = lax.broadcasted_iota(jnp.int32, (picks.shape[0], width), 1)
    total = jnp.zeros((picks.shape[0], width), jnp.float32)
    for k in range(picks.shape[1]):
        total = total + jnp.where(ids[:, k : k + 1] == lane, weight[:, k : k + 1], 0.0)
    out_ref[:, count:] = total.astype(jnp.bfloat16)


def shared_in_kernel(start_ref, x_ref, gate_ref, up_ref, out_ref):
    contract = (((1,), (1,)), ((), ()))
    block, slab = gate_ref.shape
    x = x_ref[...]
    if x.shape[1] != slab:
        x = x_ref[:, pl.ds(pl.multiple_of(start_ref[0], LANES), slab)]
    for i, ref in enumerate((gate_ref, up_ref)):
        part = lax.dot_general(x, ref[...], contract, preferred_element_type=jnp.float32)
        out_ref[:, i * block : (i + 1) * block] = part.astype(jnp.bfloat16)


def routed_kernel(near_count, first_ref, x_ref, gate_hbm, up_hbm, down_hbm, *refs):
    near, out_ref = refs[:near_count], refs[near_count]
    far_refs, sems = refs[near_count + 1 : -1], refs[-1]
    held, count, _ = gate_hbm.shape
    copies = []
    for i, there in enumerate(far_refs):
        e, kind = divmod(near_count + i, 3)
        here = (gate_hbm, up_hbm, down_hbm)[kind].at[e]
        copies.append(pltpu.make_async_copy(here, there, sems.at[i]))
        copies[-1].start()

    def fetch(index):
        if index < near_count:
            return near[index][...]
        copies[index - near_count].wait()
        return far_refs[index - near_count][...]

    x = x_ref[:, :count]
    weights = x_ref[:, count:].astype(jnp.float32)
    lane = lax.broadcasted_iota(jnp.int32, weights.shape, 1)
    for e in range(held):
        chosen = jnp.where(lane == first_ref[0] + e, weights, 0.0)
        weight = jnp.sum(chosen, axis=1, keepdims=True)
        gate = jnp.dot(x, fetch(3 * e), preferred_element_type=jnp.float32)
        up = jnp.dot(x, fetch(3 * e + 1), preferred_element_type=jnp.float32)
        hidden = (jax.nn.silu(gate) * up * weight).astype(jnp.bfloat16)
        term = jnp.dot(hidden, fetch(3 * e + 2), preferred_element_type=jnp.float32)
        if e == 0:
            out_ref[...] = term
        else:
            out_ref[...] += term


def shared_out_kernel(tokens, start_ref, routed_ref, down_ref, *refs):
    parts, out_ref = refs[:-1], refs[-1]
    block, slab = down_ref.shape
    count, width = out_ref.shape
    total = parts[0][...].astype(jnp.float32)
    to = lax.broadcasted_iota(jnp.int32, (count, count), 0)
    come = lax.broadcasted_iota(jnp.int32, (count, count), 1)
    for k in range(1, len(parts)):
        place = (come == (to ^ (k * tokens))).astype(jnp.bfloat16)
        total += jnp.dot(place, parts[k][...], preferred_element_type=jnp.float32)
    hidden = (jax.nn.silu(total[:, :block]) * total[:, block:]).astype(jnp.bfloat16)
    shared = jnp.dot(hidden, down_ref[...], preferred_element_type=jnp.float32)
    if slab == width:
        out_ref[...] = (routed_ref[...] + shared).astype(jnp.bfloat16)
    else:
        out_ref[...] = routed_ref[...].astype(jnp.bfloat16)
        columns = pl.ds(pl.multiple_of(start_ref[0], LANES), slab)
        out_ref[:, columns] = (routed_ref[:, columns] + shared).astype(jnp.bfloat16)


def bring_kernel(which, rows_ref, *refs):
    count = len(which)
    sources, kept, sems = refs[:count], refs[count:-1], refs[-1]
    copies = []
    for i, e in enumerate(which):
        here = sources[i] if e is None else sources[i].at[e]
        copies.append(pltpu.make_async_copy(here, kept[i], sems.at[i]))
        copies[-1].start()
    for copy in copies:
        copy.wait()


def bring(wanted, rows):
    hbm = pl.BlockSpec(memory_space=pl.ANY)
    shapes = [w.shape if e is None else w.shape[1:] for w, e in wanted]
    return pl.pallas_call(
        functools.partial(bring_kernel, [e for _, e in wanted]),
        out_shape=[pltpu.VMEM(shape, jnp.bfloat16) for shape in shapes],
        in_specs=[hbm] * (1 + len(wanted)),
        out_specs=[pl.BlockSpec(memory_space=pltpu.VMEM)] * len(wanted),
        scratch_shapes=[pltpu.SemaphoreType.DMA((len(wanted),))],
        compiler_params=pltpu.CompilerParams(
            vmem_limit_bytes=2 * sum(math.prod(shape) for shape in shapes) + MIB
        ),
    )(rows, *(far(w) for w, _ in wanted))


def far(value):
    return pltpu.with_memory_space_constraint(value, pltpu.HBM)


def exchange(value, axis, bit):
    size = lax.axis_size(axis)
    return lax.ppermute(value, axis, [(i, i ^ bit) for i in range(size)])


def add_rows(one, other):
    return (one.astype(jnp.float32) + other.astype(jnp.float32)).astype(jnp.bfloat16)


def local(
    hidden_states,
    norm_gain,
    route_groups,
    route_picks,
    gate_weights,
    expert_gate,
    expert_up,
    expert_down,
    shared_gate,
    shared_up,
    shared_down,
):
    node_count = lax.axis_size("node")
    local_count = lax.axis_size("local")
    node = lax.axis_index("node")
    token_count, feature_count = hidden_states.shape
    held, _, block = expert_gate.shape
    expert_total = held * node_count
    per_group = expert_total // NODE_GROUPS
    width = feature_count + -(-expert_total // LANES) * LANES
    slab = shared_gate.shape[1]
    shared_block = shared_gate.shape[0]
    row_total = token_count * node_count * local_count
    params = pltpu.CompilerParams(
        vmem_limit_bytes=4 * MIB + (12 * width + 2 * node_count * 2 * shared_block) * row_total
    )
    smem = pl.BlockSpec(memory_space=pltpu.SMEM)
    vmem = pl.BlockSpec(memory_space=pltpu.VMEM)
    hbm = pl.BlockSpec(memory_space=pl.ANY)
    small = (hidden_states, norm_gain, route_groups, route_picks, gate_weights)
    rows = pl.pallas_call(
        functools.partial(pack_kernel, per_group),
        out_shape=jax.ShapeDtypeStruct((token_count, width), jnp.bfloat16),
        in_specs=[hbm] * len(small),
        out_specs=vmem,
        scratch_shapes=[pltpu.VMEM(a.shape, a.dtype) for a in small]
        + [pltpu.SemaphoreType.DMA((len(small),))],
        compiler_params=params,
    )(*(far(a) for a in small))

    weights = [(w, e) for e in range(held) for w in (expert_gate, expert_up, expert_down)]
    stages = [("node", 1 << i) for i in range(node_count.bit_length() - 1)]
    stages += [("local", 1 << i) for i in reversed(range(local_count.bit_length() - 1))]
    ready = []
    for stage, (axis, bit) in enumerate(stages):
        other = exchange(rows, axis, bit)
        take = NEAR_PLAN[stage] if stage < len(NEAR_PLAN) else 0
        wanted = weights[len(ready) : len(ready) + take]
        extra = [(shared_gate, None), (shared_up, None)] if stage == len(stages) - 2 else []
        if wanted or extra:
            got = bring(wanted + extra, rows)
            other, *got = lax.optimization_barrier((other, *got))
            ready += got[: len(wanted)]
            if extra:
                shared_gate, shared_up = got[len(wanted) :]
        rows = jnp.concatenate([rows, other], axis=0)
    row_count = rows.shape[0]

    start = (node * slab).astype(jnp.int32)
    aligned = slab % LANES == 0
    mine = rows if aligned else lax.dynamic_slice_in_dim(rows, start, slab, axis=1)
    shared_part = pl.pallas_call(
        shared_in_kernel,
        out_shape=jax.ShapeDtypeStruct((row_count, 2 * shared_block), jnp.bfloat16),
        in_specs=[smem, vmem, vmem, vmem],
        compiler_params=params,
    )(start.reshape(1), mine, shared_gate, shared_up)
    parts = [shared_part] + [exchange(shared_part, "node", k) for k in range(1, node_count)]

    late = weights[len(ready) :]
    late_bytes = 2 * sum(math.prod(w.shape[1:]) for w, _ in late)
    routed = pl.pallas_call(
        functools.partial(routed_kernel, len(ready)),
        out_shape=jax.ShapeDtypeStruct((row_count, feature_count), jnp.float32),
        in_specs=[smem, vmem, hbm, hbm, hbm] + [vmem] * len(ready),
        out_specs=vmem,
        scratch_shapes=[pltpu.VMEM(w.shape[1:], jnp.bfloat16) for w, _ in late]
        + [pltpu.SemaphoreType.DMA((max(len(late), 1),))],
        compiler_params=pltpu.CompilerParams(
            vmem_limit_bytes=late_bytes + 12 * row_count * width + 4 * MIB
        ),
    )(
        (node * held).astype(jnp.int32).reshape(1),
        rows,
        *(far(w) for w in (expert_gate, expert_up, expert_down)),
        *ready,
    )

    if not aligned:
        shared_down = lax.dynamic_update_slice_in_dim(
            jnp.zeros((shared_block, feature_count), shared_down.dtype), shared_down, start, axis=1
        )
    out = pl.pallas_call(
        functools.partial(shared_out_kernel, token_count),
        out_shape=jax.ShapeDtypeStruct((row_count, feature_count), jnp.bfloat16),
        in_specs=[smem] + [vmem] * (2 + node_count),
        out_specs=vmem,
        compiler_params=params,
    )(start.reshape(1), routed, shared_down, *parts)

    bit = 1
    while bit < local_count:
        half = out.shape[0] // 2
        out = add_rows(out[:half], exchange(out[half:], "local", bit))
        bit *= 2
    bit = node_count // 2
    while bit:
        half = out.shape[0] // 2
        out = add_rows(out[:half], exchange(out[half:], "node", bit))
        bit //= 2
    return out


def solution(mesh):
    placed = (
        P(("groups", "node", "local"), None),
        P(),
        P(("groups", "node", "local"), None),
        P(("groups", "node", "local"), None),
        P(("groups", "node", "local"), None),
        P("node", None, "local"),
        P("node", None, "local"),
        P("node", "local", None),
        P("local", "node"),
        P("local", "node"),
        P("local", "node"),
    )
    return jax.shard_map(
        local,
        mesh=mesh,
        in_specs=placed,
        out_specs=P(("groups", "node", "local"), None),
        check_vma=False,
    )
```

```python
import functools
import math

import jax
import jax.numpy as jnp
from jax import lax
from jax.experimental import pallas as pl
from jax.experimental.pallas import tpu as pltpu
from jax.sharding import PartitionSpec as P

NODE_GROUPS = 8
LANES = 128
MIB = 2**20
NEAR_PLAN = (2, 2, 4, 1)


def pack_kernel(per_group, node_ref, *refs):
    count = len(refs) // 2 - 1
    sources, out_ref, staged, sems = refs[:count], refs[count], refs[count + 1 : -1], refs[-1]
    copies = [
        pltpu.make_async_copy(here, there, sems.at[i])
        for i, (here, there) in enumerate(zip(sources, staged))
    ]
    for copy in copies:
        copy.start()
    for copy in copies:
        copy.wait()
    x_ref, gain_ref, groups_ref, picks_ref, weight_ref = staged
    features = x_ref[...].astype(jnp.float32)
    count = features.shape[1]
    mean_square = jnp.mean(features * features, axis=1, keepdims=True)
    normed = features * lax.rsqrt(mean_square + 1e-06) * gain_ref[...].reshape(1, -1)
    out_ref[:, :count] = normed.astype(jnp.bfloat16)
    picks = picks_ref[...]
    groups = groups_ref[...]
    weight = weight_ref[...].astype(jnp.float32)
    slot = lax.div(picks, jnp.full_like(picks, per_group))
    inner = picks - slot * per_group
    group = jnp.zeros_like(picks)
    for a in range(groups.shape[1]):
        group = jnp.where(slot == a, groups[:, a : a + 1], group)
    ids = group * per_group + inner
    width = out_ref.shape[1] - count
    lane = lax.broadcasted_iota(jnp.int32, (picks.shape[0], width), 1)
    total = jnp.zeros((picks.shape[0], width), jnp.float32)
    for k in range(picks.shape[1]):
        total = total + jnp.where(ids[:, k : k + 1] == lane, weight[:, k : k + 1], 0.0)
    out_ref[:, count:] = total.astype(jnp.bfloat16)


def shared_in_kernel(node_ref, x_ref, gate_ref, up_ref, out_ref):
    contract = (((1,), (1,)), ((), ()))
    block, slab = gate_ref.shape
    x = x_ref[...]
    if x.shape[1] != slab:
        x = x_ref[:, pl.ds(pl.multiple_of(node_ref[0] * slab, LANES), slab)]
    for i, ref in enumerate((gate_ref, up_ref)):
        part = lax.dot_general(x, ref[...], contract, preferred_element_type=jnp.float32)
        out_ref[:, i * block : (i + 1) * block] = part.astype(jnp.bfloat16)


def routed_kernel(near_count, node_ref, x_ref, gate_hbm, up_hbm, down_hbm, *refs):
    near, out_ref = refs[:near_count], refs[near_count]
    far_refs, sems = refs[near_count + 1 : -1], refs[-1]
    held, count, _ = gate_hbm.shape
    copies = []
    for i, there in enumerate(far_refs):
        e, kind = divmod(near_count + i, 3)
        here = (gate_hbm, up_hbm, down_hbm)[kind].at[e]
        copies.append(pltpu.make_async_copy(here, there, sems.at[i]))
        copies[-1].start()

    def fetch(index):
        if index < near_count:
            return near[index][...]
        copies[index - near_count].wait()
        return far_refs[index - near_count][...]

    x = x_ref[:, :count]
    weights = x_ref[:, count:].astype(jnp.float32)
    lane = lax.broadcasted_iota(jnp.int32, weights.shape, 1)
    for e in range(held):
        chosen = jnp.where(lane == node_ref[0] * held + e, weights, 0.0)
        weight = jnp.sum(chosen, axis=1, keepdims=True)
        gate = jnp.dot(x, fetch(3 * e), preferred_element_type=jnp.float32)
        up = jnp.dot(x, fetch(3 * e + 1), preferred_element_type=jnp.float32)
        hidden = (jax.nn.silu(gate) * up * weight).astype(jnp.bfloat16)
        term = jnp.dot(hidden, fetch(3 * e + 2), preferred_element_type=jnp.float32)
        if e == 0:
            out_ref[...] = term
        else:
            out_ref[...] += term


def shared_out_kernel(tokens, node_ref, routed_ref, down_ref, *refs):
    parts, out_ref = refs[:-1], refs[-1]
    block, slab = down_ref.shape
    count, width = out_ref.shape
    total = parts[0][...].astype(jnp.float32)
    to = lax.broadcasted_iota(jnp.int32, (count, count), 0)
    come = lax.broadcasted_iota(jnp.int32, (count, count), 1)
    for k in range(1, len(parts)):
        place = (come == (to ^ (k * tokens))).astype(jnp.bfloat16)
        total += jnp.dot(place, parts[k][...], preferred_element_type=jnp.float32)
    hidden = (jax.nn.silu(total[:, :block]) * total[:, block:]).astype(jnp.bfloat16)
    shared = jnp.dot(hidden, down_ref[...], preferred_element_type=jnp.float32)
    if slab == width:
        out_ref[...] = (routed_ref[...] + shared).astype(jnp.bfloat16)
    else:
        out_ref[...] = routed_ref[...].astype(jnp.bfloat16)
        columns = pl.ds(pl.multiple_of(node_ref[0] * slab, LANES), slab)
        out_ref[:, columns] = (routed_ref[:, columns] + shared).astype(jnp.bfloat16)


def bring_kernel(which, rows_ref, *refs):
    count = len(which)
    sources, kept, sems = refs[:count], refs[count:-1], refs[-1]
    copies = []
    for i, e in enumerate(which):
        here = sources[i] if e is None else sources[i].at[e]
        copies.append(pltpu.make_async_copy(here, kept[i], sems.at[i]))
        copies[-1].start()
    for copy in copies:
        copy.wait()


def bring(wanted, rows):
    hbm = pl.BlockSpec(memory_space=pl.ANY)
    shapes = [w.shape if e is None else w.shape[1:] for w, e in wanted]
    return pl.pallas_call(
        functools.partial(bring_kernel, [e for _, e in wanted]),
        out_shape=[pltpu.VMEM(shape, jnp.bfloat16) for shape in shapes],
        in_specs=[hbm] * (1 + len(wanted)),
        out_specs=[pl.BlockSpec(memory_space=pltpu.VMEM)] * len(wanted),
        scratch_shapes=[pltpu.SemaphoreType.DMA((len(wanted),))],
        compiler_params=pltpu.CompilerParams(
            vmem_limit_bytes=2 * sum(math.prod(shape) for shape in shapes) + MIB
        ),
    )(rows, *(far(w) for w, _ in wanted))


def join_kernel(one_ref, other_ref, out_ref):
    both = [ref[...].astype(jnp.float32) for ref in (one_ref, other_ref)]
    out_ref[...] = jnp.concatenate(both, axis=0).astype(jnp.bfloat16)


def join(one, other):
    vmem = pl.BlockSpec(memory_space=pltpu.VMEM)
    return pl.pallas_call(
        join_kernel,
        out_shape=jax.ShapeDtypeStruct((2 * one.shape[0], one.shape[1]), one.dtype),
        in_specs=[vmem, vmem],
        out_specs=vmem,
        compiler_params=pltpu.CompilerParams(vmem_limit_bytes=24 * one.size + MIB),
    )(one, other)


def far(value):
    return pltpu.with_memory_space_constraint(value, pltpu.HBM)


def exchange(value, axis, bit):
    size = lax.axis_size(axis)
    return lax.ppermute(value, axis, [(i, i ^ bit) for i in range(size)])


def add_rows(one, other):
    return (one.astype(jnp.float32) + other.astype(jnp.float32)).astype(jnp.bfloat16)


def local(
    hidden_states,
    norm_gain,
    route_groups,
    route_picks,
    gate_weights,
    expert_gate,
    expert_up,
    expert_down,
    shared_gate,
    shared_up,
    shared_down,
):
    node_count = lax.axis_size("node")
    local_count = lax.axis_size("local")
    node = lax.axis_index("node")
    place = node.astype(jnp.int32).reshape(1)
    token_count, feature_count = hidden_states.shape
    held, _, block = expert_gate.shape
    expert_total = held * node_count
    per_group = expert_total // NODE_GROUPS
    width = feature_count + -(-expert_total // LANES) * LANES
    slab = shared_gate.shape[1]
    shared_block = shared_gate.shape[0]
    row_total = token_count * node_count * local_count
    params = pltpu.CompilerParams(
        vmem_limit_bytes=4 * MIB + (12 * width + 2 * node_count * 2 * shared_block) * row_total
    )
    smem = pl.BlockSpec(memory_space=pltpu.SMEM)
    vmem = pl.BlockSpec(memory_space=pltpu.VMEM)
    hbm = pl.BlockSpec(memory_space=pl.ANY)
    small = (hidden_states, norm_gain, route_groups, route_picks, gate_weights)
    rows = pl.pallas_call(
        functools.partial(pack_kernel, per_group),
        out_shape=jax.ShapeDtypeStruct((token_count, width), jnp.bfloat16),
        in_specs=[smem] + [hbm] * len(small),
        out_specs=vmem,
        scratch_shapes=[pltpu.VMEM(a.shape, a.dtype) for a in small]
        + [pltpu.SemaphoreType.DMA((len(small),))],
        compiler_params=params,
    )(place, *(far(a) for a in small))

    weights = [(w, e) for e in range(held) for w in (expert_gate, expert_up, expert_down)]
    stages = [("node", 1 << i) for i in range(node_count.bit_length() - 1)]
    stages += [("local", 1 << i) for i in reversed(range(local_count.bit_length() - 1))]
    ready = []
    for stage, (axis, bit) in enumerate(stages):
        other = exchange(rows, axis, bit)
        take = NEAR_PLAN[stage] if stage < len(NEAR_PLAN) else 0
        wanted = weights[len(ready) : len(ready) + take]
        extra = [(shared_gate, None), (shared_up, None)] if stage == len(stages) - 2 else []
        if wanted or extra:
            got = bring(wanted + extra, rows)
            other, *got = lax.optimization_barrier((other, *got))
            ready += got[: len(wanted)]
            if extra:
                shared_gate, shared_up = got[len(wanted) :]
        rows = join(rows, other)
    row_count = rows.shape[0]

    aligned = slab % LANES == 0
    mine = rows if aligned else lax.dynamic_slice_in_dim(rows, node * slab, slab, axis=1)
    shared_part = pl.pallas_call(
        shared_in_kernel,
        out_shape=jax.ShapeDtypeStruct((row_count, 2 * shared_block), jnp.bfloat16),
        in_specs=[smem, vmem, vmem, vmem],
        compiler_params=params,
    )(place, mine, shared_gate, shared_up)
    parts = [shared_part] + [exchange(shared_part, "node", k) for k in range(1, node_count)]

    late = weights[len(ready) :]
    late_bytes = 2 * sum(math.prod(w.shape[1:]) for w, _ in late)
    routed = pl.pallas_call(
        functools.partial(routed_kernel, len(ready)),
        out_shape=jax.ShapeDtypeStruct((row_count, feature_count), jnp.float32),
        in_specs=[smem, vmem, hbm, hbm, hbm] + [vmem] * len(ready),
        out_specs=vmem,
        scratch_shapes=[pltpu.VMEM(w.shape[1:], jnp.bfloat16) for w, _ in late]
        + [pltpu.SemaphoreType.DMA((max(len(late), 1),))],
        compiler_params=pltpu.CompilerParams(
            vmem_limit_bytes=late_bytes + 12 * row_count * width + 4 * MIB
        ),
    )(
        place,
        rows,
        *(far(w) for w in (expert_gate, expert_up, expert_down)),
        *ready,
    )

    if not aligned:
        shared_down = lax.dynamic_update_slice_in_dim(
            jnp.zeros((shared_block, feature_count), shared_down.dtype), shared_down, node * slab, axis=1
        )
    out = pl.pallas_call(
        functools.partial(shared_out_kernel, token_count),
        out_shape=jax.ShapeDtypeStruct((row_count, feature_count), jnp.bfloat16),
        in_specs=[smem] + [vmem] * (2 + node_count),
        out_specs=vmem,
        compiler_params=params,
    )(place, routed, shared_down, *parts)

    bit = 1
    while bit < local_count:
        half = out.shape[0] // 2
        out = add_rows(out[:half], exchange(out[half:], "local", bit))
        bit *= 2
    bit = node_count // 2
    while bit:
        half = out.shape[0] // 2
        out = add_rows(out[:half], exchange(out[half:], "node", bit))
        bit //= 2
    return out


def solution(mesh):
    placed = (
        P(("groups", "node", "local"), None),
        P(),
        P(("groups", "node", "local"), None),
        P(("groups", "node", "local"), None),
        P(("groups", "node", "local"), None),
        P("node", None, "local"),
        P("node", None, "local"),
        P("node", "local", None),
        P("local", "node"),
        P("local", "node"),
        P("local", "node"),
    )
    return jax.shard_map(
        local,
        mesh=mesh,
        in_specs=placed,
        out_specs=P(("groups", "node", "local"), None),
        check_vma=False,
    )
```

```python
import functools
import math

import jax
import jax.numpy as jnp
from jax import lax
from jax.experimental import pallas as pl
from jax.experimental.pallas import tpu as pltpu
from jax.sharding import PartitionSpec as P

NODE_GROUPS = 8
LANES = 128
MIB = 2**20
NEAR_PLAN = (0, 0, 4, 1)
WORTH = 40 * 10**9


def pack_kernel(per_group, node_ref, *refs):
    count = len(refs) // 2 - 1
    sources, out_ref, staged, sems = refs[:count], refs[count], refs[count + 1 : -1], refs[-1]
    copies = [
        pltpu.make_async_copy(here, there, sems.at[i])
        for i, (here, there) in enumerate(zip(sources, staged))
    ]
    for copy in copies:
        copy.start()
    for copy in copies:
        copy.wait()
    x_ref, gain_ref, groups_ref, picks_ref, weight_ref = staged
    features = x_ref[...].astype(jnp.float32)
    count = features.shape[1]
    mean_square = jnp.mean(features * features, axis=1, keepdims=True)
    normed = features * lax.rsqrt(mean_square + 1e-06) * gain_ref[...].reshape(1, -1)
    out_ref[:, :count] = normed.astype(jnp.bfloat16)
    picks = picks_ref[...]
    groups = groups_ref[...]
    weight = weight_ref[...].astype(jnp.float32)
    slot = lax.div(picks, jnp.full_like(picks, per_group))
    inner = picks - slot * per_group
    group = jnp.zeros_like(picks)
    for a in range(groups.shape[1]):
        group = jnp.where(slot == a, groups[:, a : a + 1], group)
    ids = group * per_group + inner
    width = out_ref.shape[1] - count
    lane = lax.broadcasted_iota(jnp.int32, (picks.shape[0], width), 1)
    total = jnp.zeros((picks.shape[0], width), jnp.float32)
    for k in range(picks.shape[1]):
        total = total + jnp.where(ids[:, k : k + 1] == lane, weight[:, k : k + 1], 0.0)
    out_ref[:, count:] = total.astype(jnp.bfloat16)


def shared_in_kernel(node_ref, x_ref, gate_ref, up_ref, out_ref):
    contract = (((1,), (1,)), ((), ()))
    block, slab = gate_ref.shape
    x = x_ref[...]
    if x.shape[1] != slab:
        x = x_ref[:, pl.ds(pl.multiple_of(node_ref[0] * slab, LANES), slab)]
    for i, ref in enumerate((gate_ref, up_ref)):
        part = lax.dot_general(x, ref[...], contract, preferred_element_type=jnp.float32)
        out_ref[:, i * block : (i + 1) * block] = part.astype(jnp.bfloat16)


def routed_kernel(near_count, node_ref, x_ref, gate_hbm, up_ref, down_ref, *refs):
    near_refs, out_ref = refs[:near_count], refs[near_count]
    far_refs, sems = refs[near_count + 1 : -1], refs[-1]
    held, count, _ = up_ref.shape
    copies = []
    for i, there in enumerate(far_refs):
        copies.append(pltpu.make_async_copy(gate_hbm.at[near_count + i], there, sems.at[i]))
        copies[-1].start()

    x = x_ref[:, :count]
    weights = x_ref[:, count:].astype(jnp.float32)
    lane = lax.broadcasted_iota(jnp.int32, weights.shape, 1)

    def gate_and_up(e):
        if e < near_count:
            gate_ref = near_refs[e]
        else:
            gate_ref = far_refs[e - near_count]
            copies[e - near_count].wait()
        return [
            jnp.dot(x, weight, preferred_element_type=jnp.float32)
            for weight in (gate_ref[...], up_ref[e])
        ]

    gate, up = gate_and_up(0)
    for e in range(held):
        chosen = jnp.where(lane == node_ref[0] * held + e, weights, 0.0)
        weight = jnp.sum(chosen, axis=1, keepdims=True)
        if e + 1 < held:
            later = gate_and_up(e + 1)
        hidden = (jax.nn.silu(gate) * up * weight).astype(jnp.bfloat16)
        term = jnp.dot(hidden, down_ref[e], preferred_element_type=jnp.float32)
        if e == 0:
            out_ref[...] = term
        else:
            out_ref[...] += term
        if e + 1 < held:
            gate, up = later


def shared_out_kernel(tokens, node_ref, routed_ref, down_ref, *refs):
    parts, out_ref = refs[:-1], refs[-1]
    block, slab = down_ref.shape
    count, width = out_ref.shape
    total = parts[0][...].astype(jnp.float32)
    to = lax.broadcasted_iota(jnp.int32, (count, count), 0)
    come = lax.broadcasted_iota(jnp.int32, (count, count), 1)
    for k in range(1, len(parts)):
        place = (come == (to ^ (k * tokens))).astype(jnp.bfloat16)
        total += jnp.dot(place, parts[k][...], preferred_element_type=jnp.float32)
    hidden = (jax.nn.silu(total[:, :block]) * total[:, block:]).astype(jnp.bfloat16)
    shared = jnp.dot(hidden, down_ref[...], preferred_element_type=jnp.float32)
    if slab == width:
        out_ref[...] = (routed_ref[...] + shared).astype(jnp.bfloat16)
    else:
        out_ref[...] = routed_ref[...].astype(jnp.bfloat16)
        columns = pl.ds(pl.multiple_of(node_ref[0] * slab, LANES), slab)
        out_ref[:, columns] = (routed_ref[:, columns] + shared).astype(jnp.bfloat16)


def bring_kernel(which, rows_ref, *refs):
    count = len(which)
    sources, kept, sems = refs[:count], refs[count:-1], refs[-1]
    copies = []
    for i, e in enumerate(which):
        here = sources[i] if e is None else sources[i].at[e]
        copies.append(pltpu.make_async_copy(here, kept[i], sems.at[i]))
        copies[-1].start()
    for copy in copies:
        copy.wait()


def bring(wanted, rows):
    hbm = pl.BlockSpec(memory_space=pl.ANY)
    shapes = [w.shape if e is None else w.shape[1:] for w, e in wanted]
    return pl.pallas_call(
        functools.partial(bring_kernel, [e for _, e in wanted]),
        out_shape=[pltpu.VMEM(shape, jnp.bfloat16) for shape in shapes],
        in_specs=[hbm] * (1 + len(wanted)),
        out_specs=[pl.BlockSpec(memory_space=pltpu.VMEM)] * len(wanted),
        scratch_shapes=[pltpu.SemaphoreType.DMA((len(wanted),))],
        compiler_params=pltpu.CompilerParams(
            vmem_limit_bytes=2 * sum(math.prod(shape) for shape in shapes) + MIB
        ),
    )(rows, *(far(w) for w, _ in wanted))


def join_kernel(one_ref, other_ref, out_ref):
    both = [ref[...].astype(jnp.float32) for ref in (one_ref, other_ref)]
    out_ref[...] = jnp.concatenate(both, axis=0).astype(jnp.bfloat16)


def join(one, other):
    vmem = pl.BlockSpec(memory_space=pltpu.VMEM)
    return pl.pallas_call(
        join_kernel,
        out_shape=jax.ShapeDtypeStruct((2 * one.shape[0], one.shape[1]), one.dtype),
        in_specs=[vmem, vmem],
        out_specs=vmem,
        compiler_params=pltpu.CompilerParams(vmem_limit_bytes=24 * one.size + MIB),
    )(one, other)


def near(value):
    return pltpu.with_memory_space_constraint(value, pltpu.VMEM)


def far(value):
    return pltpu.with_memory_space_constraint(value, pltpu.HBM)


def exchange(value, axis, bit):
    size = lax.axis_size(axis)
    return lax.ppermute(value, axis, [(i, i ^ bit) for i in range(size)])


def add_rows(one, other):
    return (one.astype(jnp.float32) + other.astype(jnp.float32)).astype(jnp.bfloat16)


def local(
    hidden_states,
    norm_gain,
    route_groups,
    route_picks,
    gate_weights,
    expert_gate,
    expert_up,
    expert_down,
    shared_gate,
    shared_up,
    shared_down,
):
    node_count = lax.axis_size("node")
    local_count = lax.axis_size("local")
    node = lax.axis_index("node")
    place = node.astype(jnp.int32).reshape(1)
    token_count, feature_count = hidden_states.shape
    held, _, block = expert_gate.shape
    expert_total = held * node_count
    per_group = expert_total // NODE_GROUPS
    width = feature_count + -(-expert_total // LANES) * LANES
    slab = shared_gate.shape[1]
    shared_block = shared_gate.shape[0]
    row_total = token_count * node_count * local_count
    params = pltpu.CompilerParams(
        vmem_limit_bytes=4 * MIB + (12 * width + 2 * node_count * 2 * shared_block) * row_total
    )
    smem = pl.BlockSpec(memory_space=pltpu.SMEM)
    vmem = pl.BlockSpec(memory_space=pltpu.VMEM)
    hbm = pl.BlockSpec(memory_space=pl.ANY)
    small = (hidden_states, norm_gain, route_groups, route_picks, gate_weights)
    rows = pl.pallas_call(
        functools.partial(pack_kernel, per_group),
        out_shape=jax.ShapeDtypeStruct((token_count, width), jnp.bfloat16),
        in_specs=[smem] + [hbm] * len(small),
        out_specs=vmem,
        scratch_shapes=[pltpu.VMEM(a.shape, a.dtype) for a in small]
        + [pltpu.SemaphoreType.DMA((len(small),))],
        compiler_params=params,
        cost_estimate=pl.CostEstimate(flops=WORTH, transcendentals=0, bytes_accessed=0),
    )(place, *(far(a) for a in small))

    weights = [(expert_gate, e) for e in range(held)]
    stages = [("node", 1 << i) for i in range(node_count.bit_length() - 1)]
    stages += [("local", 1 << i) for i in reversed(range(local_count.bit_length() - 1))]
    ready = []
    for stage, (axis, bit) in enumerate(stages):
        other = exchange(rows, axis, bit)
        take = NEAR_PLAN[stage] if stage < len(NEAR_PLAN) else 0
        wanted = weights[len(ready) : len(ready) + take]
        extra = [(shared_gate, None), (shared_up, None)] if stage == len(stages) - 2 else []
        if wanted or extra:
            got = bring(wanted + extra, rows)
            other, *got = lax.optimization_barrier((other, *got))
            ready += got[: len(wanted)]
            if extra:
                shared_gate, shared_up = got[len(wanted) :]
        rows = join(rows, other)
    row_count = rows.shape[0]

    aligned = slab % LANES == 0
    mine = rows if aligned else lax.dynamic_slice_in_dim(rows, node * slab, slab, axis=1)
    shared_part = pl.pallas_call(
        shared_in_kernel,
        out_shape=jax.ShapeDtypeStruct((row_count, 2 * shared_block), jnp.bfloat16),
        in_specs=[smem, vmem, vmem, vmem],
        compiler_params=params,
    )(place, mine, shared_gate, shared_up)
    parts = [shared_part] + [exchange(shared_part, "node", k) for k in range(1, node_count)]

    late = weights[len(ready) :]
    late_bytes = 2 * sum(math.prod(w.shape[1:]) for w, _ in late)
    routed = pl.pallas_call(
        functools.partial(routed_kernel, len(ready)),
        out_shape=jax.ShapeDtypeStruct((row_count, feature_count), jnp.float32),
        in_specs=[smem, vmem, hbm, vmem, vmem] + [vmem] * len(ready),
        out_specs=vmem,
        scratch_shapes=[pltpu.VMEM(w.shape[1:], jnp.bfloat16) for w, _ in late]
        + [pltpu.SemaphoreType.DMA((max(len(late), 1),))],
        compiler_params=pltpu.CompilerParams(
            vmem_limit_bytes=late_bytes + 12 * row_count * width + 4 * MIB
        ),
    )(
        place,
        rows,
        far(expert_gate),
        near(expert_up),
        near(expert_down),
        *ready,
    )

    if not aligned:
        shared_down = lax.dynamic_update_slice_in_dim(
            jnp.zeros((shared_block, feature_count), shared_down.dtype), shared_down, node * slab, axis=1
        )
    out = pl.pallas_call(
        functools.partial(shared_out_kernel, token_count),
        out_shape=jax.ShapeDtypeStruct((row_count, feature_count), jnp.bfloat16),
        in_specs=[smem] + [vmem] * (2 + node_count),
        out_specs=vmem,
        compiler_params=params,
    )(place, routed, shared_down, *parts)

    bit = 1
    while bit < local_count:
        half = out.shape[0] // 2
        out = add_rows(out[:half], exchange(out[half:], "local", bit))
        bit *= 2
    bit = node_count // 2
    while bit:
        half = out.shape[0] // 2
        out = add_rows(out[:half], exchange(out[half:], "node", bit))
        bit //= 2
    return out


def solution(mesh):
    placed = (
        P(("groups", "node", "local"), None),
        P(),
        P(("groups", "node", "local"), None),
        P(("groups", "node", "local"), None),
        P(("groups", "node", "local"), None),
        P("node", None, "local"),
        P("node", None, "local"),
        P("node", "local", None),
        P("local", "node"),
        P("local", "node"),
        P("local", "node"),
    )
    return jax.shard_map(
        local,
        mesh=mesh,
        in_specs=placed,
        out_specs=P(("groups", "node", "local"), None),
        check_vma=False,
    )
```

```python
import functools
import math

import jax
import jax.numpy as jnp
from jax import lax
from jax.experimental import pallas as pl
from jax.experimental.pallas import tpu as pltpu
from jax.sharding import PartitionSpec as P

NODE_GROUPS = 8
LANES = 128
MIB = 2**20
NEAR_PLAN = (0, 4, 1)
DIRECT = 4
WORTH = 40 * 10**9


def pack_kernel(per_group, node_ref, *refs):
    count = len(refs) // 2 - 1
    sources, out_ref, staged, sems = refs[:count], refs[count], refs[count + 1 : -1], refs[-1]
    copies = [
        pltpu.make_async_copy(here, there, sems.at[i])
        for i, (here, there) in enumerate(zip(sources, staged))
    ]
    for copy in copies:
        copy.start()
    for copy in copies:
        copy.wait()
    x_ref, gain_ref, groups_ref, picks_ref, weight_ref = staged
    features = x_ref[...].astype(jnp.float32)
    count = features.shape[1]
    mean_square = jnp.mean(features * features, axis=1, keepdims=True)
    normed = features * lax.rsqrt(mean_square + 1e-06) * gain_ref[...].reshape(1, -1)
    out_ref[:, :count] = normed.astype(jnp.bfloat16)
    picks = picks_ref[...]
    groups = groups_ref[...]
    weight = weight_ref[...].astype(jnp.float32)
    slot = lax.div(picks, jnp.full_like(picks, per_group))
    inner = picks - slot * per_group
    group = jnp.zeros_like(picks)
    for a in range(groups.shape[1]):
        group = jnp.where(slot == a, groups[:, a : a + 1], group)
    ids = group * per_group + inner
    width = out_ref.shape[1] - count
    lane = lax.broadcasted_iota(jnp.int32, (picks.shape[0], width), 1)
    total = jnp.zeros((picks.shape[0], width), jnp.float32)
    for k in range(picks.shape[1]):
        total = total + jnp.where(ids[:, k : k + 1] == lane, weight[:, k : k + 1], 0.0)
    out_ref[:, count:] = total.astype(jnp.bfloat16)


def shared_in_kernel(node_ref, x_ref, gate_ref, up_ref, out_ref):
    contract = (((1,), (1,)), ((), ()))
    block, slab = gate_ref.shape
    x = x_ref[...]
    if x.shape[1] != slab:
        x = x_ref[:, pl.ds(pl.multiple_of(node_ref[0] * slab, LANES), slab)]
    for i, ref in enumerate((gate_ref, up_ref)):
        part = lax.dot_general(x, ref[...], contract, preferred_element_type=jnp.float32)
        out_ref[:, i * block : (i + 1) * block] = part.astype(jnp.bfloat16)


def routed_kernel(near_count, node_ref, x_ref, gate_hbm, up_ref, down_ref, *refs):
    near_refs, out_ref = refs[:near_count], refs[near_count]
    far_refs, sems = refs[near_count + 1 : -1], refs[-1]
    held, count, _ = up_ref.shape
    copies = []
    for i, there in enumerate(far_refs):
        copies.append(pltpu.make_async_copy(gate_hbm.at[near_count + i], there, sems.at[i]))
        copies[-1].start()

    x = x_ref[:, :count]
    weights = x_ref[:, count:].astype(jnp.float32)
    lane = lax.broadcasted_iota(jnp.int32, weights.shape, 1)

    def gate_and_up(e):
        if e < near_count:
            gate_ref = near_refs[e]
        else:
            gate_ref = far_refs[e - near_count]
            copies[e - near_count].wait()
        return [
            jnp.dot(x, weight, preferred_element_type=jnp.float32)
            for weight in (gate_ref[...], up_ref[e])
        ]

    gate, up = gate_and_up(0)
    for e in range(held):
        chosen = jnp.where(lane == node_ref[0] * held + e, weights, 0.0)
        weight = jnp.sum(chosen, axis=1, keepdims=True)
        if e + 1 < held:
            later = gate_and_up(e + 1)
        hidden = (jax.nn.silu(gate) * up * weight).astype(jnp.bfloat16)
        term = jnp.dot(hidden, down_ref[e], preferred_element_type=jnp.float32)
        if e == 0:
            out_ref[...] = term
        else:
            out_ref[...] += term
        if e + 1 < held:
            gate, up = later


def shared_out_kernel(unit, node_ref, routed_ref, down_ref, *refs):
    parts, out_ref = refs[:-1], refs[-1]
    block, slab = down_ref.shape
    count, width = out_ref.shape
    total = parts[0][...].astype(jnp.float32)
    to = lax.broadcasted_iota(jnp.int32, (count, count), 0)
    come = lax.broadcasted_iota(jnp.int32, (count, count), 1)
    for k in range(1, len(parts)):
        place = (come == (to ^ (k * unit))).astype(jnp.bfloat16)
        total += jnp.dot(place, parts[k][...], preferred_element_type=jnp.float32)
    hidden = (jax.nn.silu(total[:, :block]) * total[:, block:]).astype(jnp.bfloat16)
    shared = jnp.dot(hidden, down_ref[...], preferred_element_type=jnp.float32)
    if slab == width:
        out_ref[...] = (routed_ref[...] + shared).astype(jnp.bfloat16)
    else:
        out_ref[...] = routed_ref[...].astype(jnp.bfloat16)
        columns = pl.ds(pl.multiple_of(node_ref[0] * slab, LANES), slab)
        out_ref[:, columns] = (routed_ref[:, columns] + shared).astype(jnp.bfloat16)


def bring_kernel(which, rows_ref, *refs):
    count = len(which)
    sources, kept, sems = refs[:count], refs[count:-1], refs[-1]
    copies = []
    for i, e in enumerate(which):
        here = sources[i] if e is None else sources[i].at[e]
        copies.append(pltpu.make_async_copy(here, kept[i], sems.at[i]))
        copies[-1].start()
    for copy in copies:
        copy.wait()


def bring(wanted, rows):
    hbm = pl.BlockSpec(memory_space=pl.ANY)
    shapes = [w.shape if e is None else w.shape[1:] for w, e in wanted]
    return pl.pallas_call(
        functools.partial(bring_kernel, [e for _, e in wanted]),
        out_shape=[pltpu.VMEM(shape, jnp.bfloat16) for shape in shapes],
        in_specs=[hbm] * (1 + len(wanted)),
        out_specs=[pl.BlockSpec(memory_space=pltpu.VMEM)] * len(wanted),
        scratch_shapes=[pltpu.SemaphoreType.DMA((len(wanted),))],
        compiler_params=pltpu.CompilerParams(
            vmem_limit_bytes=2 * sum(math.prod(shape) for shape in shapes) + MIB
        ),
    )(rows, *(far(w) for w, _ in wanted))


def join_kernel(*refs):
    rows = [ref[...].astype(jnp.float32) for ref in refs[:-1]]
    refs[-1][...] = jnp.concatenate(rows, axis=0).astype(jnp.bfloat16)


def join(*pieces):
    vmem = pl.BlockSpec(memory_space=pltpu.VMEM)
    count, width = pieces[0].shape
    return pl.pallas_call(
        join_kernel,
        out_shape=jax.ShapeDtypeStruct((len(pieces) * count, width), pieces[0].dtype),
        in_specs=[vmem] * len(pieces),
        out_specs=vmem,
        compiler_params=pltpu.CompilerParams(
            vmem_limit_bytes=12 * len(pieces) * count * width + MIB
        ),
    )(*pieces)


def near(value):
    return pltpu.with_memory_space_constraint(value, pltpu.VMEM)


def far(value):
    return pltpu.with_memory_space_constraint(value, pltpu.HBM)


def exchange(value, axis, bit):
    size = lax.axis_size(axis)
    return lax.ppermute(value, axis, [(i, i ^ bit) for i in range(size)])


def local(
    hidden_states,
    norm_gain,
    route_groups,
    route_picks,
    gate_weights,
    expert_gate,
    expert_up,
    expert_down,
    shared_gate,
    shared_up,
    shared_down,
):
    node_count = lax.axis_size("node")
    local_count = lax.axis_size("local")
    node = lax.axis_index("node")
    place = node.astype(jnp.int32).reshape(1)
    token_count, feature_count = hidden_states.shape
    held, _, block = expert_gate.shape
    expert_total = held * node_count
    per_group = expert_total // NODE_GROUPS
    width = feature_count + -(-expert_total // LANES) * LANES
    slab = shared_gate.shape[1]
    shared_block = shared_gate.shape[0]
    row_total = token_count * node_count * local_count
    params = pltpu.CompilerParams(
        vmem_limit_bytes=4 * MIB + (12 * width + 2 * node_count * 2 * shared_block) * row_total
    )
    smem = pl.BlockSpec(memory_space=pltpu.SMEM)
    vmem = pl.BlockSpec(memory_space=pltpu.VMEM)
    hbm = pl.BlockSpec(memory_space=pl.ANY)
    small = (hidden_states, norm_gain, route_groups, route_picks, gate_weights)
    rows = pl.pallas_call(
        functools.partial(pack_kernel, per_group),
        out_shape=jax.ShapeDtypeStruct((token_count, width), jnp.bfloat16),
        in_specs=[smem] + [hbm] * len(small),
        out_specs=vmem,
        scratch_shapes=[pltpu.VMEM(a.shape, a.dtype) for a in small]
        + [pltpu.SemaphoreType.DMA((len(small),))],
        compiler_params=params,
        cost_estimate=pl.CostEstimate(flops=WORTH, transcendentals=0, bytes_accessed=0),
    )(place, *(far(a) for a in small))

    weights = [(expert_gate, e) for e in range(held)]
    halves = [("local", (1 << i,)) for i in reversed(range(local_count.bit_length() - 1))]
    if node_count <= DIRECT:
        stages = halves[:-1] + [("node", tuple(range(1, node_count)))] + halves[-1:]
    else:
        doubling = [("node", (1 << i,)) for i in range(node_count.bit_length() - 1)]
        stages = halves[:-1] + doubling + halves[-1:]
    node_unit = token_count << max(len(halves) - 1, 0)
    ready = []
    for stage, (axis, bits) in enumerate(stages):
        others = [exchange(rows, axis, bit) for bit in bits]
        take = NEAR_PLAN[stage] if stage < len(NEAR_PLAN) else 0
        wanted = weights[len(ready) : len(ready) + take]
        extra = [(shared_gate, None), (shared_up, None)] if stage == len(stages) - 2 else []
        if wanted or extra:
            got = bring(wanted + extra, rows)
            others, got = lax.optimization_barrier((others, got))
            ready += got[: len(wanted)]
            if extra:
                shared_gate, shared_up = got[len(wanted) :]
        rows = join(rows, *others)
    row_count = rows.shape[0]

    aligned = slab % LANES == 0
    mine = rows if aligned else lax.dynamic_slice_in_dim(rows, node * slab, slab, axis=1)
    shared_part = pl.pallas_call(
        shared_in_kernel,
        out_shape=jax.ShapeDtypeStruct((row_count, 2 * shared_block), jnp.bfloat16),
        in_specs=[smem, vmem, vmem, vmem],
        compiler_params=params,
    )(place, mine, shared_gate, shared_up)
    parts = [shared_part] + [exchange(shared_part, "node", k) for k in range(1, node_count)]

    late = weights[len(ready) :]
    late_bytes = 2 * sum(math.prod(w.shape[1:]) for w, _ in late)
    routed = pl.pallas_call(
        functools.partial(routed_kernel, len(ready)),
        out_shape=jax.ShapeDtypeStruct((row_count, feature_count), jnp.float32),
        in_specs=[smem, vmem, hbm, vmem, vmem] + [vmem] * len(ready),
        out_specs=vmem,
        scratch_shapes=[pltpu.VMEM(w.shape[1:], jnp.bfloat16) for w, _ in late]
        + [pltpu.SemaphoreType.DMA((max(len(late), 1),))],
        compiler_params=pltpu.CompilerParams(
            vmem_limit_bytes=late_bytes + 12 * row_count * width + 4 * MIB
        ),
    )(
        place,
        rows,
        far(expert_gate),
        near(expert_up),
        near(expert_down),
        *ready,
    )

    if not aligned:
        shared_down = lax.dynamic_update_slice_in_dim(
            jnp.zeros((shared_block, feature_count), shared_down.dtype), shared_down, node * slab, axis=1
        )
    out = pl.pallas_call(
        functools.partial(shared_out_kernel, node_unit),
        out_shape=jax.ShapeDtypeStruct((row_count, feature_count), jnp.bfloat16),
        in_specs=[smem] + [vmem] * (2 + node_count),
        out_specs=vmem,
        compiler_params=params,
    )(place, routed, shared_down, *parts)

    for axis, bits in reversed(stages):
        unit = out.shape[0] // (len(bits) + 1)
        total = out[:unit].astype(jnp.float32)
        for i in reversed(range(len(bits))):
            piece = out[unit * (i + 1) : unit * (i + 2)]
            total = total + exchange(piece, axis, bits[i]).astype(jnp.float32)
        out = total.astype(jnp.bfloat16)
    return out


def solution(mesh):
    placed = (
        P(("groups", "node", "local"), None),
        P(),
        P(("groups", "node", "local"), None),
        P(("groups", "node", "local"), None),
        P(("groups", "node", "local"), None),
        P("node", None, "local"),
        P("node", None, "local"),
        P("node", "local", None),
        P("local", "node"),
        P("local", "node"),
        P("local", "node"),
    )
    return jax.shard_map(
        local,
        mesh=mesh,
        in_specs=placed,
        out_specs=P(("groups", "node", "local"), None),
        check_vma=False,
    )
```

```python
import functools
import math

import jax
import jax.numpy as jnp
from jax import lax
from jax.experimental import pallas as pl
from jax.experimental.pallas import tpu as pltpu
from jax.sharding import PartitionSpec as P

NODE_GROUPS = 8
LANES = 128
MIB = 2**20
NEAR_PLAN = (0, 4, 0)
DIRECT = 4
WORTH = 40 * 10**9


def pack_kernel(per_group, node_ref, *refs):
    count = len(refs) // 2 - 1
    sources, out_ref, staged, sems = refs[:count], refs[count], refs[count + 1 : -1], refs[-1]
    copies = [
        pltpu.make_async_copy(here, there, sems.at[i])
        for i, (here, there) in enumerate(zip(sources, staged))
    ]
    for copy in copies:
        copy.start()
    for copy in copies:
        copy.wait()
    x_ref, gain_ref, groups_ref, picks_ref, weight_ref = staged
    features = x_ref[...].astype(jnp.float32)
    count = features.shape[1]
    mean_square = jnp.mean(features * features, axis=1, keepdims=True)
    normed = features * lax.rsqrt(mean_square + 1e-06) * gain_ref[...].reshape(1, -1)
    out_ref[:, :count] = normed.astype(jnp.bfloat16)
    picks = picks_ref[...]
    groups = groups_ref[...]
    weight = weight_ref[...].astype(jnp.float32)
    slot = lax.div(picks, jnp.full_like(picks, per_group))
    inner = picks - slot * per_group
    group = jnp.zeros_like(picks)
    for a in range(groups.shape[1]):
        group = jnp.where(slot == a, groups[:, a : a + 1], group)
    ids = group * per_group + inner
    width = out_ref.shape[1] - count
    lane = lax.broadcasted_iota(jnp.int32, (picks.shape[0], width), 1)
    total = jnp.zeros((picks.shape[0], width), jnp.float32)
    for k in range(picks.shape[1]):
        total = total + jnp.where(ids[:, k : k + 1] == lane, weight[:, k : k + 1], 0.0)
    out_ref[:, count:] = total.astype(jnp.bfloat16)


def shared_in_kernel(node_ref, x_ref, *refs):
    weights, out_ref = refs[:-1], refs[-1]
    contract = (((1,), (1,)), ((), ()))
    block, slab = weights[0].shape
    x = x_ref[...]
    if x.shape[1] != slab:
        x = x_ref[:, pl.ds(pl.multiple_of(node_ref[0] * slab, LANES), slab)]
    for i, ref in enumerate(weights):
        part = lax.dot_general(x, ref[...], contract, preferred_element_type=jnp.float32)
        out_ref[:, i * block : (i + 1) * block] = part.astype(jnp.bfloat16)


def routed_kernel(near_count, node_ref, x_ref, gate_hbm, up_ref, down_ref, *refs):
    near_refs, (keep_ref, send_ref) = refs[:near_count], refs[near_count : near_count + 2]
    far_refs, out_ref, sems = refs[near_count + 2 : -2], refs[-2], refs[-1]
    held, count, _ = up_ref.shape
    copies = []
    for i, there in enumerate(far_refs):
        copies.append(pltpu.make_async_copy(gate_hbm.at[near_count + i], there, sems.at[i]))
        copies[-1].start()

    x = x_ref[:, :count]
    weights = x_ref[:, count:].astype(jnp.float32)
    lane = lax.broadcasted_iota(jnp.int32, weights.shape, 1)

    def gate_and_up(e):
        if e < near_count:
            gate_ref = near_refs[e]
        else:
            gate_ref = far_refs[e - near_count]
            copies[e - near_count].wait()
        return [
            jnp.dot(x, weight, preferred_element_type=jnp.float32)
            for weight in (gate_ref[...], up_ref[e])
        ]

    gate, up = gate_and_up(0)
    for e in range(held):
        chosen = jnp.where(lane == node_ref[0] * held + e, weights, 0.0)
        weight = jnp.sum(chosen, axis=1, keepdims=True)
        if e + 1 < held:
            later = gate_and_up(e + 1)
        hidden = (jax.nn.silu(gate) * up * weight).astype(jnp.bfloat16)
        term = jnp.dot(hidden, down_ref[e], preferred_element_type=jnp.float32)
        if e == 0:
            out_ref[...] = term
        else:
            out_ref[...] += term
        if e + 1 < held:
            gate, up = later
    half = keep_ref.shape[0]
    keep_ref[...] = out_ref[:half, :]
    send_ref[...] = out_ref[half:, :].astype(jnp.bfloat16)


def shared_out_kernel(unit, node_ref, routed_ref, *refs):
    downs, parts, out_ref = refs[:2], refs[2:-1], refs[-1]
    block, slab = downs[0].shape
    count, width = out_ref.shape
    total = parts[0][...].astype(jnp.float32)
    to = lax.broadcasted_iota(jnp.int32, (count, count), 0)
    come = lax.broadcasted_iota(jnp.int32, (count, count), 1)
    for k in range(1, len(parts)):
        place = (come == (to ^ (k * unit))).astype(jnp.bfloat16)
        total += jnp.dot(place, parts[k][...], preferred_element_type=jnp.float32)
    shared = jnp.zeros((count, slab), jnp.float32)
    for i, down_ref in enumerate(downs):
        gate = total[:, 2 * i * block : (2 * i + 1) * block]
        up = total[:, (2 * i + 1) * block : (2 * i + 2) * block]
        hidden = (jax.nn.silu(gate) * up).astype(jnp.bfloat16)
        shared += jnp.dot(hidden, down_ref[...], preferred_element_type=jnp.float32)
    if slab == width:
        out_ref[...] = routed_ref[...] + shared
    else:
        out_ref[...] = routed_ref[...]
        columns = pl.ds(pl.multiple_of(node_ref[0] * slab, LANES), slab)
        out_ref[:, columns] = routed_ref[:, columns] + shared


def bring_kernel(which, rows_ref, *refs):
    count = len(which)
    sources, kept, sems = refs[:count], refs[count:-1], refs[-1]
    copies = []
    for i, e in enumerate(which):
        here = sources[i] if e is None else sources[i].at[e]
        copies.append(pltpu.make_async_copy(here, kept[i], sems.at[i]))
        copies[-1].start()
    for copy in copies:
        copy.wait()


def bring(wanted, rows):
    hbm = pl.BlockSpec(memory_space=pl.ANY)
    shapes = [w.shape if e is None else w.shape[1:] for w, e in wanted]
    return pl.pallas_call(
        functools.partial(bring_kernel, [e for _, e in wanted]),
        out_shape=[pltpu.VMEM(shape, jnp.bfloat16) for shape in shapes],
        in_specs=[hbm] * (1 + len(wanted)),
        out_specs=[pl.BlockSpec(memory_space=pltpu.VMEM)] * len(wanted),
        scratch_shapes=[pltpu.SemaphoreType.DMA((len(wanted),))],
        compiler_params=pltpu.CompilerParams(
            vmem_limit_bytes=2 * sum(math.prod(shape) for shape in shapes) + MIB
        ),
    )(rows, *(far(w) for w, _ in wanted))


def join_kernel(*refs):
    rows = [ref[...].astype(jnp.float32) for ref in refs[:-1]]
    refs[-1][...] = jnp.concatenate(rows, axis=0).astype(jnp.bfloat16)


def join(*pieces):
    vmem = pl.BlockSpec(memory_space=pltpu.VMEM)
    count, width = pieces[0].shape
    return pl.pallas_call(
        join_kernel,
        out_shape=jax.ShapeDtypeStruct((len(pieces) * count, width), pieces[0].dtype),
        in_specs=[vmem] * len(pieces),
        out_specs=vmem,
        compiler_params=pltpu.CompilerParams(
            vmem_limit_bytes=12 * len(pieces) * count * width + MIB
        ),
    )(*pieces)


def near(value):
    return pltpu.with_memory_space_constraint(value, pltpu.VMEM)


def far(value):
    return pltpu.with_memory_space_constraint(value, pltpu.HBM)


def exchange(value, axis, bit):
    size = lax.axis_size(axis)
    return lax.ppermute(value, axis, [(i, i ^ bit) for i in range(size)])


def local(
    hidden_states,
    norm_gain,
    route_groups,
    route_picks,
    gate_weights,
    expert_gate,
    expert_up,
    expert_down,
    shared_gate,
    shared_up,
    shared_down,
):
    node_count = lax.axis_size("node")
    local_count = lax.axis_size("local")
    node = lax.axis_index("node")
    place = node.astype(jnp.int32).reshape(1)
    token_count, feature_count = hidden_states.shape
    held, _, block = expert_gate.shape
    expert_total = held * node_count
    per_group = expert_total // NODE_GROUPS
    width = feature_count + -(-expert_total // LANES) * LANES
    slab = shared_gate.shape[1]
    shared_block = shared_gate.shape[0]
    row_total = token_count * node_count * local_count
    params = pltpu.CompilerParams(
        vmem_limit_bytes=4 * MIB + (12 * width + 2 * node_count * 2 * shared_block) * row_total
    )
    smem = pl.BlockSpec(memory_space=pltpu.SMEM)
    vmem = pl.BlockSpec(memory_space=pltpu.VMEM)
    hbm = pl.BlockSpec(memory_space=pl.ANY)
    small = (hidden_states, norm_gain, route_groups, route_picks, gate_weights)
    rows = pl.pallas_call(
        functools.partial(pack_kernel, per_group),
        out_shape=jax.ShapeDtypeStruct((token_count, width), jnp.bfloat16),
        in_specs=[smem] + [hbm] * len(small),
        out_specs=vmem,
        scratch_shapes=[pltpu.VMEM(a.shape, a.dtype) for a in small]
        + [pltpu.SemaphoreType.DMA((len(small),))],
        compiler_params=params,
        cost_estimate=pl.CostEstimate(flops=WORTH, transcendentals=0, bytes_accessed=0),
    )(place, *(far(a) for a in small))

    weights = [(expert_gate, e) for e in range(held)]
    halves = [("local", (1 << i,)) for i in reversed(range(local_count.bit_length() - 1))]
    if node_count <= DIRECT:
        stages = halves[:-1] + [("node", tuple(range(1, node_count)))] + halves[-1:]
    else:
        doubling = [("node", (1 << i,)) for i in range(node_count.bit_length() - 1)]
        stages = halves[:-1] + doubling + halves[-1:]
    node_unit = token_count << max(len(halves) - 1, 0)
    aligned = slab % LANES == 0
    shared_pair = [exchange(w, "local", 1) for w in (shared_gate, shared_up, shared_down)]
    ready = []
    for stage, (axis, bits) in enumerate(stages):
        others = [exchange(rows, axis, bit) for bit in bits]
        take = NEAR_PLAN[stage] if stage < len(NEAR_PLAN) else 0
        wanted = weights[len(ready) : len(ready) + take]
        extra = [(shared_gate, None), (shared_up, None)] if stage == len(stages) - 2 else []
        if wanted or extra:
            got = bring(wanted + extra, rows)
            others, got = lax.optimization_barrier((others, got))
            ready += got[: len(wanted)]
            if extra:
                shared_gate, shared_up = got[len(wanted) :]
        if stage == len(stages) - 1:
            mine = rows
            if not aligned:
                mine = lax.dynamic_slice_in_dim(rows, node * slab, slab, axis=1)
            shared_part = pl.pallas_call(
                shared_in_kernel,
                out_shape=jax.ShapeDtypeStruct((rows.shape[0], 4 * shared_block), jnp.bfloat16),
                in_specs=[smem] + [vmem] * 5,
                compiler_params=params,
            )(place, mine, shared_gate, shared_up, *shared_pair[:2])
            others, shared_part = lax.optimization_barrier((others, shared_part))
            parts = [exchange(shared_part, "node", k) for k in range(1, node_count)]
            parts = [shared_part] + parts
        rows = join(rows, *others)
    row_count = rows.shape[0]

    late = weights[len(ready) :]
    late_bytes = 2 * sum(math.prod(w.shape[1:]) for w, _ in late)
    half_shape = (row_count // 2, feature_count)
    kept, sent = pl.pallas_call(
        functools.partial(routed_kernel, len(ready)),
        out_shape=[
            jax.ShapeDtypeStruct(half_shape, jnp.float32),
            jax.ShapeDtypeStruct(half_shape, jnp.bfloat16),
        ],
        in_specs=[smem, vmem, hbm, vmem, vmem] + [vmem] * len(ready),
        out_specs=[vmem, vmem],
        scratch_shapes=[pltpu.VMEM(w.shape[1:], jnp.bfloat16) for w, _ in late]
        + [
            pltpu.VMEM((row_count, feature_count), jnp.float32),
            pltpu.SemaphoreType.DMA((max(len(late), 1),)),
        ],
        compiler_params=pltpu.CompilerParams(
            vmem_limit_bytes=late_bytes + 16 * row_count * width + 4 * MIB
        ),
    )(
        place,
        rows,
        far(expert_gate),
        near(expert_up),
        near(expert_down),
        *ready,
    )

    downs = [shared_down, shared_pair[2]]
    if not aligned:
        wide = jnp.zeros((shared_block, feature_count), shared_down.dtype)
        downs = [lax.dynamic_update_slice_in_dim(wide, w, node * slab, axis=1) for w in downs]
    kept, sent, parts = lax.optimization_barrier((kept, sent, parts))
    came = exchange(sent, "local", 1)
    kept = pl.pallas_call(
        functools.partial(shared_out_kernel, node_unit),
        out_shape=jax.ShapeDtypeStruct(kept.shape, jnp.float32),
        in_specs=[smem] + [vmem] * (3 + node_count),
        out_specs=vmem,
        compiler_params=params,
    )(place, kept, *downs, *parts)
    out = (kept + came.astype(jnp.float32)).astype(jnp.bfloat16)

    for axis, bits in reversed(stages[:-1]):
        unit = out.shape[0] // (len(bits) + 1)
        total = out[:unit].astype(jnp.float32)
        for i in reversed(range(len(bits))):
            piece = out[unit * (i + 1) : unit * (i + 2)]
            total = total + exchange(piece, axis, bits[i]).astype(jnp.float32)
        out = total.astype(jnp.bfloat16)
    return out


def solution(mesh):
    placed = (
        P(("groups", "node", "local"), None),
        P(),
        P(("groups", "node", "local"), None),
        P(("groups", "node", "local"), None),
        P(("groups", "node", "local"), None),
        P("node", None, "local"),
        P("node", None, "local"),
        P("node", "local", None),
        P("local", "node"),
        P("local", "node"),
        P("local", "node"),
    )
    return jax.shard_map(
        local,
        mesh=mesh,
        in_specs=placed,
        out_specs=P(("groups", "node", "local"), None),
        check_vma=False,
    )
```

```python
import functools
import math

import jax
import jax.numpy as jnp
from jax import lax
from jax.experimental import pallas as pl
from jax.experimental.pallas import tpu as pltpu
from jax.sharding import PartitionSpec as P

NODE_GROUPS = 8
LANES = 128
MIB = 2**20
NEAR_PLAN = (0, 4, 0)
DIRECT = 4
WORTH = 80 * 10**9


def pack_kernel(per_group, node_ref, *refs):
    count = len(refs) // 2 - 1
    sources, out_ref, staged, sems = refs[:count], refs[count], refs[count + 1 : -1], refs[-1]
    copies = [
        pltpu.make_async_copy(here, there, sems.at[i])
        for i, (here, there) in enumerate(zip(sources, staged))
    ]
    for copy in copies:
        copy.start()
    for copy in copies:
        copy.wait()
    x_ref, gain_ref, groups_ref, picks_ref, weight_ref = staged
    features = x_ref[...].astype(jnp.float32)
    count = features.shape[1]
    mean_square = jnp.mean(features * features, axis=1, keepdims=True)
    normed = features * lax.rsqrt(mean_square + 1e-06) * gain_ref[...].reshape(1, -1)
    out_ref[:, :count] = normed.astype(jnp.bfloat16)
    picks = picks_ref[...]
    groups = groups_ref[...]
    weight = weight_ref[...].astype(jnp.float32)
    slot = lax.div(picks, jnp.full_like(picks, per_group))
    inner = picks - slot * per_group
    group = jnp.zeros_like(picks)
    for a in range(groups.shape[1]):
        group = jnp.where(slot == a, groups[:, a : a + 1], group)
    ids = group * per_group + inner
    width = out_ref.shape[1] - count
    lane = lax.broadcasted_iota(jnp.int32, (picks.shape[0], width), 1)
    total = jnp.zeros((picks.shape[0], width), jnp.float32)
    for k in range(picks.shape[1]):
        total = total + jnp.where(ids[:, k : k + 1] == lane, weight[:, k : k + 1], 0.0)
    out_ref[:, count:] = total.astype(jnp.bfloat16)


def shared_in_kernel(node_ref, x_ref, *refs):
    weights, out_ref = refs[:-1], refs[-1]
    contract = (((1,), (1,)), ((), ()))
    block, slab = weights[0].shape
    x = x_ref[...]
    if x.shape[1] != slab:
        x = x_ref[:, pl.ds(pl.multiple_of(node_ref[0] * slab, LANES), slab)]
    for i, ref in enumerate(weights):
        part = lax.dot_general(x, ref[...], contract, preferred_element_type=jnp.float32)
        out_ref[:, i * block : (i + 1) * block] = part.astype(jnp.bfloat16)


def routed_kernel(near_count, node_ref, x_ref, gate_hbm, up_ref, down_ref, *refs):
    near_refs, (keep_ref, send_ref) = refs[:near_count], refs[near_count : near_count + 2]
    far_refs, out_ref, sems = refs[near_count + 2 : -2], refs[-2], refs[-1]
    held, count, _ = up_ref.shape
    copies = []
    for i, there in enumerate(far_refs):
        copies.append(pltpu.make_async_copy(gate_hbm.at[near_count + i], there, sems.at[i]))
        copies[-1].start()

    x = x_ref[:, :count]
    weights = x_ref[:, count:].astype(jnp.float32)
    lane = lax.broadcasted_iota(jnp.int32, weights.shape, 1)

    def gate_and_up(e):
        if e < near_count:
            gate_ref = near_refs[e]
        else:
            gate_ref = far_refs[e - near_count]
            copies[e - near_count].wait()
        return [
            jnp.dot(x, weight, preferred_element_type=jnp.float32)
            for weight in (gate_ref[...], up_ref[e])
        ]

    gate, up = gate_and_up(0)
    for e in range(held):
        chosen = jnp.where(lane == node_ref[0] * held + e, weights, 0.0)
        weight = jnp.sum(chosen, axis=1, keepdims=True)
        if e + 1 < held:
            later = gate_and_up(e + 1)
        hidden = (jax.nn.silu(gate) * up * weight).astype(jnp.bfloat16)
        term = jnp.dot(hidden, down_ref[e], preferred_element_type=jnp.float32)
        if e == 0:
            out_ref[...] = term
        else:
            out_ref[...] += term
        if e + 1 < held:
            gate, up = later
    half = keep_ref.shape[0]
    keep_ref[...] = out_ref[:half, :]
    send_ref[...] = out_ref[half:, :].astype(jnp.bfloat16)


def shared_out_kernel(unit, node_ref, routed_ref, *refs):
    downs, parts, out_ref = refs[:2], refs[2:-1], refs[-1]
    block, slab = downs[0].shape
    count, width = out_ref.shape
    total = parts[0][...].astype(jnp.float32)
    to = lax.broadcasted_iota(jnp.int32, (count, count), 0)
    come = lax.broadcasted_iota(jnp.int32, (count, count), 1)
    for k in range(1, len(parts)):
        place = (come == (to ^ (k * unit))).astype(jnp.bfloat16)
        total += jnp.dot(place, parts[k][...], preferred_element_type=jnp.float32)
    shared = jnp.zeros((count, slab), jnp.float32)
    for i, down_ref in enumerate(downs):
        gate = total[:, 2 * i * block : (2 * i + 1) * block]
        up = total[:, (2 * i + 1) * block : (2 * i + 2) * block]
        hidden = (jax.nn.silu(gate) * up).astype(jnp.bfloat16)
        shared += jnp.dot(hidden, down_ref[...], preferred_element_type=jnp.float32)
    if slab == width:
        out_ref[...] = routed_ref[...] + shared
    else:
        out_ref[...] = routed_ref[...]
        columns = pl.ds(pl.multiple_of(node_ref[0] * slab, LANES), slab)
        out_ref[:, columns] = routed_ref[:, columns] + shared


def bring_kernel(which, rows_ref, *refs):
    count = len(which)
    sources, kept, sems = refs[:count], refs[count:-1], refs[-1]
    copies = []
    for i, e in enumerate(which):
        here = sources[i] if e is None else sources[i].at[e]
        copies.append(pltpu.make_async_copy(here, kept[i], sems.at[i]))
        copies[-1].start()
    for copy in copies:
        copy.wait()


def bring(wanted, rows):
    hbm = pl.BlockSpec(memory_space=pl.ANY)
    shapes = [w.shape if e is None else w.shape[1:] for w, e in wanted]
    return pl.pallas_call(
        functools.partial(bring_kernel, [e for _, e in wanted]),
        out_shape=[pltpu.VMEM(shape, jnp.bfloat16) for shape in shapes],
        in_specs=[hbm] * (1 + len(wanted)),
        out_specs=[pl.BlockSpec(memory_space=pltpu.VMEM)] * len(wanted),
        scratch_shapes=[pltpu.SemaphoreType.DMA((len(wanted),))],
        compiler_params=pltpu.CompilerParams(
            vmem_limit_bytes=2 * sum(math.prod(shape) for shape in shapes) + MIB
        ),
    )(rows, *(far(w) for w, _ in wanted))


def join_kernel(*refs):
    rows = [ref[...].astype(jnp.float32) for ref in refs[:-1]]
    refs[-1][...] = jnp.concatenate(rows, axis=0).astype(jnp.bfloat16)


def join(*pieces):
    vmem = pl.BlockSpec(memory_space=pltpu.VMEM)
    count, width = pieces[0].shape
    return pl.pallas_call(
        join_kernel,
        out_shape=jax.ShapeDtypeStruct((len(pieces) * count, width), pieces[0].dtype),
        in_specs=[vmem] * len(pieces),
        out_specs=vmem,
        compiler_params=pltpu.CompilerParams(
            vmem_limit_bytes=12 * len(pieces) * count * width + MIB
        ),
    )(*pieces)


def near(value):
    return pltpu.with_memory_space_constraint(value, pltpu.VMEM)


def far(value):
    return pltpu.with_memory_space_constraint(value, pltpu.HBM)


def exchange(value, axis, bit):
    size = lax.axis_size(axis)
    return lax.ppermute(value, axis, [(i, i ^ bit) for i in range(size)])


def local(
    hidden_states,
    norm_gain,
    route_groups,
    route_picks,
    gate_weights,
    expert_gate,
    expert_up,
    expert_down,
    shared_gate,
    shared_up,
    shared_down,
):
    node_count = lax.axis_size("node")
    local_count = lax.axis_size("local")
    node = lax.axis_index("node")
    place = node.astype(jnp.int32).reshape(1)
    token_count, feature_count = hidden_states.shape
    held, _, block = expert_gate.shape
    expert_total = held * node_count
    per_group = expert_total // NODE_GROUPS
    width = feature_count + -(-expert_total // LANES) * LANES
    slab = shared_gate.shape[1]
    shared_block = shared_gate.shape[0]
    row_total = token_count * node_count * local_count
    params = pltpu.CompilerParams(
        vmem_limit_bytes=4 * MIB + (12 * width + 2 * node_count * 2 * shared_block) * row_total
    )
    smem = pl.BlockSpec(memory_space=pltpu.SMEM)
    vmem = pl.BlockSpec(memory_space=pltpu.VMEM)
    hbm = pl.BlockSpec(memory_space=pl.ANY)
    small = (hidden_states, norm_gain, route_groups, route_picks, gate_weights)
    rows = pl.pallas_call(
        functools.partial(pack_kernel, per_group),
        out_shape=jax.ShapeDtypeStruct((token_count, width), jnp.bfloat16),
        in_specs=[smem] + [hbm] * len(small),
        out_specs=vmem,
        scratch_shapes=[pltpu.VMEM(a.shape, a.dtype) for a in small]
        + [pltpu.SemaphoreType.DMA((len(small),))],
        compiler_params=params,
        cost_estimate=pl.CostEstimate(flops=WORTH, transcendentals=0, bytes_accessed=0),
    )(place, *(far(a) for a in small))

    weights = [(expert_gate, e) for e in range(held)]
    halves = [("local", (1 << i,)) for i in reversed(range(local_count.bit_length() - 1))]
    if node_count <= DIRECT:
        stages = halves[:-1] + [("node", tuple(range(1, node_count)))] + halves[-1:]
    else:
        doubling = [("node", (1 << i,)) for i in range(node_count.bit_length() - 1)]
        stages = halves[:-1] + doubling + halves[-1:]
    node_unit = token_count << max(len(halves) - 1, 0)
    aligned = slab % LANES == 0
    shared_pair = [exchange(w, "local", 1) for w in (shared_gate, shared_up, shared_down)]
    ready = []
    for stage, (axis, bits) in enumerate(stages):
        others = [exchange(rows, axis, bit) for bit in bits]
        take = NEAR_PLAN[stage] if stage < len(NEAR_PLAN) else 0
        wanted = weights[len(ready) : len(ready) + take]
        extra = [(shared_gate, None), (shared_up, None)] if stage == len(stages) - 2 else []
        if wanted or extra:
            got = bring(wanted + extra, rows)
            others, got = lax.optimization_barrier((others, got))
            ready += got[: len(wanted)]
            if extra:
                shared_gate, shared_up = got[len(wanted) :]
        if stage == len(stages) - 1:
            mine = rows
            if not aligned:
                mine = lax.dynamic_slice_in_dim(rows, node * slab, slab, axis=1)
            shared_part = pl.pallas_call(
                shared_in_kernel,
                out_shape=jax.ShapeDtypeStruct((rows.shape[0], 4 * shared_block), jnp.bfloat16),
                in_specs=[smem] + [vmem] * 5,
                compiler_params=params,
            )(place, mine, shared_gate, shared_up, *shared_pair[:2])
            parts = [exchange(shared_part, "node", k) for k in range(1, node_count)]
            others, shared_part = lax.optimization_barrier((others, shared_part))
            parts = [shared_part] + parts
        rows = join(rows, *others)
    row_count = rows.shape[0]

    late = weights[len(ready) :]
    late_bytes = 2 * sum(math.prod(w.shape[1:]) for w, _ in late)
    half_shape = (row_count // 2, feature_count)
    kept, sent = pl.pallas_call(
        functools.partial(routed_kernel, len(ready)),
        out_shape=[
            jax.ShapeDtypeStruct(half_shape, jnp.float32),
            jax.ShapeDtypeStruct(half_shape, jnp.bfloat16),
        ],
        in_specs=[smem, vmem, hbm, vmem, vmem] + [vmem] * len(ready),
        out_specs=[vmem, vmem],
        scratch_shapes=[pltpu.VMEM(w.shape[1:], jnp.bfloat16) for w, _ in late]
        + [
            pltpu.VMEM((row_count, feature_count), jnp.float32),
            pltpu.SemaphoreType.DMA((max(len(late), 1),)),
        ],
        compiler_params=pltpu.CompilerParams(
            vmem_limit_bytes=late_bytes + 16 * row_count * width + 4 * MIB
        ),
    )(
        place,
        rows,
        far(expert_gate),
        near(expert_up),
        near(expert_down),
        *ready,
    )

    downs = [shared_down, shared_pair[2]]
    if not aligned:
        wide = jnp.zeros((shared_block, feature_count), shared_down.dtype)
        downs = [lax.dynamic_update_slice_in_dim(wide, w, node * slab, axis=1) for w in downs]
    kept, sent, parts = lax.optimization_barrier((kept, sent, parts))
    came = exchange(sent, "local", 1)
    kept = pl.pallas_call(
        functools.partial(shared_out_kernel, node_unit),
        out_shape=jax.ShapeDtypeStruct(kept.shape, jnp.float32),
        in_specs=[smem] + [vmem] * (3 + node_count),
        out_specs=vmem,
        compiler_params=params,
    )(place, kept, *downs, *parts)
    out = (kept + came.astype(jnp.float32)).astype(jnp.bfloat16)

    for axis, bits in reversed(stages[:-1]):
        unit = out.shape[0] // (len(bits) + 1)
        total = out[:unit].astype(jnp.float32)
        for i in reversed(range(len(bits))):
            piece = out[unit * (i + 1) : unit * (i + 2)]
            total = total + exchange(piece, axis, bits[i]).astype(jnp.float32)
        out = total.astype(jnp.bfloat16)
    return out


def solution(mesh):
    placed = (
        P(("groups", "node", "local"), None),
        P(),
        P(("groups", "node", "local"), None),
        P(("groups", "node", "local"), None),
        P(("groups", "node", "local"), None),
        P("node", None, "local"),
        P("node", None, "local"),
        P("node", "local", None),
        P("local", "node"),
        P("local", "node"),
        P("local", "node"),
    )
    return jax.shard_map(
        local,
        mesh=mesh,
        in_specs=placed,
        out_specs=P(("groups", "node", "local"), None),
        check_vma=False,
    )
```

```python
import functools
import math

import jax
import jax.numpy as jnp
from jax import lax
from jax.experimental import pallas as pl
from jax.experimental.pallas import tpu as pltpu
from jax.sharding import PartitionSpec as P

NODE_GROUPS = 8
LANES = 128
MIB = 2**20
NEAR_PLAN = (0, 4, 0)
DIRECT = 4
WORTH = 80 * 10**9


def pack_kernel(per_group, node_ref, *refs):
    count = len(refs) // 2 - 1
    sources, out_ref, staged, sems = refs[:count], refs[count], refs[count + 1 : -1], refs[-1]
    copies = [
        pltpu.make_async_copy(here, there, sems.at[i])
        for i, (here, there) in enumerate(zip(sources, staged))
    ]
    for copy in copies:
        copy.start()
    for copy in copies:
        copy.wait()
    x_ref, gain_ref, groups_ref, picks_ref, weight_ref = staged
    features = x_ref[...].astype(jnp.float32)
    count = features.shape[1]
    mean_square = jnp.mean(features * features, axis=1, keepdims=True)
    normed = features * lax.rsqrt(mean_square + 1e-06) * gain_ref[...].reshape(1, -1)
    out_ref[:, :count] = normed.astype(jnp.bfloat16)
    picks = picks_ref[...]
    groups = groups_ref[...]
    weight = weight_ref[...].astype(jnp.float32)
    slot = lax.div(picks, jnp.full_like(picks, per_group))
    inner = picks - slot * per_group
    group = jnp.zeros_like(picks)
    for a in range(groups.shape[1]):
        group = jnp.where(slot == a, groups[:, a : a + 1], group)
    ids = group * per_group + inner
    width = out_ref.shape[1] - count
    lane = lax.broadcasted_iota(jnp.int32, (picks.shape[0], width), 1)
    total = jnp.zeros((picks.shape[0], width), jnp.float32)
    for k in range(picks.shape[1]):
        total = total + jnp.where(ids[:, k : k + 1] == lane, weight[:, k : k + 1], 0.0)
    out_ref[:, count:] = total.astype(jnp.bfloat16)


def shared_in_kernel(node_ref, x_ref, *refs):
    weights, out_ref = refs[:-1], refs[-1]
    contract = (((1,), (1,)), ((), ()))
    block, slab = weights[0].shape
    x = x_ref[...]
    if x.shape[1] != slab:
        x = x_ref[:, pl.ds(pl.multiple_of(node_ref[0] * slab, LANES), slab)]
    for i, ref in enumerate(weights):
        part = lax.dot_general(x, ref[...], contract, preferred_element_type=jnp.float32)
        out_ref[:, i * block : (i + 1) * block] = part.astype(jnp.bfloat16)


def routed_kernel(near_count, node_ref, x_ref, gate_hbm, up_ref, down_ref, *refs):
    near_refs, (keep_ref, send_ref) = refs[:near_count], refs[near_count : near_count + 2]
    far_refs, out_ref, sems = refs[near_count + 2 : -2], refs[-2], refs[-1]
    held, count, _ = up_ref.shape
    copies = []
    for i, there in enumerate(far_refs):
        copies.append(pltpu.make_async_copy(gate_hbm.at[near_count + i], there, sems.at[i]))
        copies[-1].start()

    x = x_ref[:, :count]
    weights = x_ref[:, count:].astype(jnp.float32)
    lane = lax.broadcasted_iota(jnp.int32, weights.shape, 1)

    def gate_and_up(e):
        if e < near_count:
            gate_ref = near_refs[e]
        else:
            gate_ref = far_refs[e - near_count]
            copies[e - near_count].wait()
        return [
            jnp.dot(x, weight, preferred_element_type=jnp.float32)
            for weight in (gate_ref[...], up_ref[e])
        ]

    gate, up = gate_and_up(0)
    for e in range(held):
        chosen = jnp.where(lane == node_ref[0] * held + e, weights, 0.0)
        weight = jnp.sum(chosen, axis=1, keepdims=True)
        if e + 1 < held:
            later = gate_and_up(e + 1)
        hidden = (jax.nn.silu(gate) * up * weight).astype(jnp.bfloat16)
        term = jnp.dot(hidden, down_ref[e], preferred_element_type=jnp.float32)
        if e == 0:
            out_ref[...] = term
        else:
            out_ref[...] += term
        if e + 1 < held:
            gate, up = later
    half = keep_ref.shape[0]
    keep_ref[...] = out_ref[:half, :]
    send_ref[...] = out_ref[half:, :].astype(jnp.bfloat16)


def shared_out_kernel(unit, node_ref, routed_ref, *refs):
    downs, parts, out_ref = refs[:2], refs[2:-1], refs[-1]
    block, slab = downs[0].shape
    count, width = out_ref.shape
    total = parts[0][...].astype(jnp.float32)
    to = lax.broadcasted_iota(jnp.int32, (count, count), 0)
    come = lax.broadcasted_iota(jnp.int32, (count, count), 1)
    for k in range(1, len(parts)):
        place = (come == (to ^ (k * unit))).astype(jnp.bfloat16)
        total += jnp.dot(place, parts[k][...], preferred_element_type=jnp.float32)
    shared = jnp.zeros((count, slab), jnp.float32)
    for i, down_ref in enumerate(downs):
        gate = total[:, 2 * i * block : (2 * i + 1) * block]
        up = total[:, (2 * i + 1) * block : (2 * i + 2) * block]
        hidden = (jax.nn.silu(gate) * up).astype(jnp.bfloat16)
        shared += jnp.dot(hidden, down_ref[...], preferred_element_type=jnp.float32)
    if slab == width:
        out_ref[...] = routed_ref[...] + shared
    else:
        out_ref[...] = routed_ref[...]
        columns = pl.ds(pl.multiple_of(node_ref[0] * slab, LANES), slab)
        out_ref[:, columns] = routed_ref[:, columns] + shared


def bring_kernel(which, rows_ref, *refs):
    count = len(which)
    sources, kept, sems = refs[:count], refs[count:-1], refs[-1]
    copies = []
    for i, e in enumerate(which):
        here = sources[i] if e is None else sources[i].at[e]
        copies.append(pltpu.make_async_copy(here, kept[i], sems.at[i]))
        copies[-1].start()
    for copy in copies:
        copy.wait()


def bring(wanted, rows):
    hbm = pl.BlockSpec(memory_space=pl.ANY)
    shapes = [w.shape if e is None else w.shape[1:] for w, e in wanted]
    return pl.pallas_call(
        functools.partial(bring_kernel, [e for _, e in wanted]),
        out_shape=[pltpu.VMEM(shape, jnp.bfloat16) for shape in shapes],
        in_specs=[hbm] * (1 + len(wanted)),
        out_specs=[pl.BlockSpec(memory_space=pltpu.VMEM)] * len(wanted),
        scratch_shapes=[pltpu.SemaphoreType.DMA((len(wanted),))],
        compiler_params=pltpu.CompilerParams(
            vmem_limit_bytes=2 * sum(math.prod(shape) for shape in shapes) + MIB
        ),
    )(rows, *(far(w) for w, _ in wanted))


def join_kernel(*refs):
    rows = [ref[...].astype(jnp.float32) for ref in refs[:-1]]
    refs[-1][...] = jnp.concatenate(rows, axis=0).astype(jnp.bfloat16)


def join(*pieces):
    vmem = pl.BlockSpec(memory_space=pltpu.VMEM)
    count, width = pieces[0].shape
    return pl.pallas_call(
        join_kernel,
        out_shape=jax.ShapeDtypeStruct((len(pieces) * count, width), pieces[0].dtype),
        in_specs=[vmem] * len(pieces),
        out_specs=vmem,
        compiler_params=pltpu.CompilerParams(
            vmem_limit_bytes=12 * len(pieces) * count * width + MIB
        ),
    )(*pieces)


def near(value):
    return pltpu.with_memory_space_constraint(value, pltpu.VMEM)


def far(value):
    return pltpu.with_memory_space_constraint(value, pltpu.HBM)


def exchange(value, axis, bit):
    size = lax.axis_size(axis)
    return lax.ppermute(value, axis, [(i, i ^ bit) for i in range(size)])


def local(
    hidden_states,
    norm_gain,
    route_groups,
    route_picks,
    gate_weights,
    expert_gate,
    expert_up,
    expert_down,
    shared_gate,
    shared_up,
    shared_down,
):
    node_count = lax.axis_size("node")
    local_count = lax.axis_size("local")
    node = lax.axis_index("node")
    place = node.astype(jnp.int32).reshape(1)
    token_count, feature_count = hidden_states.shape
    held, _, block = expert_gate.shape
    expert_total = held * node_count
    per_group = expert_total // NODE_GROUPS
    width = feature_count + -(-expert_total // LANES) * LANES
    slab = shared_gate.shape[1]
    shared_block = shared_gate.shape[0]
    row_total = token_count * node_count * local_count
    params = pltpu.CompilerParams(
        vmem_limit_bytes=4 * MIB + (12 * width + 2 * node_count * 2 * shared_block) * row_total
    )
    smem = pl.BlockSpec(memory_space=pltpu.SMEM)
    vmem = pl.BlockSpec(memory_space=pltpu.VMEM)
    hbm = pl.BlockSpec(memory_space=pl.ANY)
    small = (hidden_states, norm_gain, route_groups, route_picks, gate_weights)
    rows = pl.pallas_call(
        functools.partial(pack_kernel, per_group),
        out_shape=jax.ShapeDtypeStruct((token_count, width), jnp.bfloat16),
        in_specs=[smem] + [hbm] * len(small),
        out_specs=vmem,
        scratch_shapes=[pltpu.VMEM(a.shape, a.dtype) for a in small]
        + [pltpu.SemaphoreType.DMA((len(small),))],
        compiler_params=params,
        cost_estimate=pl.CostEstimate(flops=WORTH, transcendentals=0, bytes_accessed=0),
    )(place, *(far(a) for a in small))

    weights = [(expert_gate, e) for e in range(held)]
    halves = [("local", (1 << i,)) for i in reversed(range(local_count.bit_length() - 1))]
    if node_count <= DIRECT:
        stages = halves[:-1] + [("node", tuple(range(1, node_count)))] + halves[-1:]
    else:
        doubling = [("node", (1 << i,)) for i in range(node_count.bit_length() - 1)]
        stages = halves[:-1] + doubling + halves[-1:]
    node_unit = token_count << max(len(halves) - 1, 0)
    aligned = slab % LANES == 0
    shared_pair = [exchange(w, "local", 1) for w in (shared_gate, shared_up, shared_down)]
    ready = []
    for stage, (axis, bits) in enumerate(stages):
        others = [exchange(rows, axis, bit) for bit in bits]
        take = NEAR_PLAN[stage] if stage < len(NEAR_PLAN) else 0
        wanted = weights[len(ready) : len(ready) + take]
        extra = [(shared_gate, None), (shared_up, None)] if stage == len(stages) - 2 else []
        if wanted or extra:
            got = bring(wanted + extra, rows)
            others, got = lax.optimization_barrier((others, got))
            ready += got[: len(wanted)]
            if extra:
                shared_gate, shared_up = got[len(wanted) :]
        if stage == len(stages) - 1:
            mine = rows
            if not aligned:
                mine = lax.dynamic_slice_in_dim(rows, node * slab, slab, axis=1)
            shared_part = pl.pallas_call(
                shared_in_kernel,
                out_shape=jax.ShapeDtypeStruct((rows.shape[0], 4 * shared_block), jnp.bfloat16),
                in_specs=[smem] + [vmem] * 5,
                compiler_params=params,
            )(place, mine, shared_gate, shared_up, *shared_pair[:2])
            parts = [exchange(shared_part, "node", k) for k in range(1, node_count)]
            others, shared_part = lax.optimization_barrier((others, shared_part))
            parts = [shared_part] + parts
        rows = join(rows, *others)
    row_count = rows.shape[0]

    late = weights[len(ready) :]
    late_bytes = 2 * sum(math.prod(w.shape[1:]) for w, _ in late)
    half_shape = (row_count // 2, feature_count)
    kept, sent = pl.pallas_call(
        functools.partial(routed_kernel, len(ready)),
        out_shape=[
            jax.ShapeDtypeStruct(half_shape, jnp.float32),
            jax.ShapeDtypeStruct(half_shape, jnp.bfloat16),
        ],
        in_specs=[smem, vmem, hbm, vmem, vmem] + [vmem] * len(ready),
        out_specs=[vmem, vmem],
        scratch_shapes=[pltpu.VMEM(w.shape[1:], jnp.bfloat16) for w, _ in late]
        + [
            pltpu.VMEM((row_count, feature_count), jnp.float32),
            pltpu.SemaphoreType.DMA((max(len(late), 1),)),
        ],
        compiler_params=pltpu.CompilerParams(
            vmem_limit_bytes=late_bytes + 16 * row_count * width + 4 * MIB
        ),
    )(
        place,
        rows,
        far(expert_gate),
        near(expert_up),
        near(expert_down),
        *ready,
    )

    downs = [shared_down, shared_pair[2]]
    if not aligned:
        wide = jnp.zeros((shared_block, feature_count), shared_down.dtype)
        downs = [lax.dynamic_update_slice_in_dim(wide, w, node * slab, axis=1) for w in downs]
    kept, sent, parts = lax.optimization_barrier((kept, sent, parts))
    came = exchange(sent, "local", 1)
    kept = pl.pallas_call(
        functools.partial(shared_out_kernel, node_unit),
        out_shape=jax.ShapeDtypeStruct(kept.shape, jnp.float32),
        in_specs=[smem] + [vmem] * (3 + node_count),
        out_specs=vmem,
        compiler_params=params,
    )(place, kept, *downs, *parts)
    out = (kept + came.astype(jnp.float32)).astype(jnp.bfloat16)

    for axis, bits in reversed(stages[:-1]):
        unit = out.shape[0] // (len(bits) + 1)
        total = out[:unit].astype(jnp.float32)
        for i in ([1, 2, 0] if len(bits) == 3 else reversed(range(len(bits)))):
            piece = out[unit * (i + 1) : unit * (i + 2)]
            total = total + exchange(piece, axis, bits[i]).astype(jnp.float32)
        out = total.astype(jnp.bfloat16)
    return out


def solution(mesh):
    placed = (
        P(("groups", "node", "local"), None),
        P(),
        P(("groups", "node", "local"), None),
        P(("groups", "node", "local"), None),
        P(("groups", "node", "local"), None),
        P("node", None, "local"),
        P("node", None, "local"),
        P("node", "local", None),
        P("local", "node"),
        P("local", "node"),
        P("local", "node"),
    )
    return jax.shard_map(
        local,
        mesh=mesh,
        in_specs=placed,
        out_specs=P(("groups", "node", "local"), None),
        check_vma=False,
    )
```
